32 devices in a mesh: run: 4 (over z), tm: 2 (over core), blk: 4 (over y, x).
Axes of the slice: x: 2, y: 2, z: 4, core: 2. Of those that a mesh axis runs over, the one named last changes fastest.
Arguments:
- series: bfloat16 [4, 1200, 6144], P('run', 'tm', 'blk'), may hold values from -60 to 60
- weights: int32 [4, 1200], P('run'), may hold values from 0 to 2
- taps: bfloat16 [33], replicated, may hold values from -3 to 3
- lags: int32 [6144], P('blk'), may hold values from 0 to 3
Outputs:
- connectome: float32 [512, 6144], P(('run', 'tm'), 'blk')
The draws below stay inside these ranges and needn't reach their ends.
All inputs are finite; a program needn't handle non-finite values.
Results may differ from the reference program's by a relative error of at most 0.00055.
Values may be sent and summed in bfloat16 or wider, within the bound.
A program may use at most 128 MiB of HBM per device.

```python
import jax
import jax.numpy as jnp
from jax import lax

FRAMES = 1200
HALF = 16
LAGS = 4
COL_DEV = 1536
SEED_DEV = 128
RUNS = 4
COLS = 6144
ROWS = 512
N_BLK = 4


def draw_series(key, part):
    key_common, key_load, key_noise, key_scale = jax.random.split(key, 4)
    common = jax.random.normal(key_common, (RUNS, FRAMES, 1), jnp.float32)
    loading = jax.random.uniform(key_load, (1, 1, COLS), jnp.float32, -1.2, 1.2)
    noise = jax.random.normal(key_noise, (RUNS, FRAMES, COLS), jnp.float32)
    scaling = jnp.exp(jax.random.uniform(key_scale, (1, 1, COLS), jnp.float32, 0.0, 1.4))
    values = jnp.clip((common * loading + noise) * scaling, -30.0, 30.0)
    return values.astype(jnp.bfloat16)


def plant(values, stream_key, least, high):
    place = [jax.random.randint(jax.random.fold_in(stream_key, axis), (), 0, length) for axis, length in enumerate(values.shape)]
    main_axis = values.shape.index(max(values.shape))
    neighbour = place[:main_axis] + [(place[main_axis] + 1) % values.shape[main_axis]] + place[main_axis + 1:]
    return values.at[tuple(place)].set(least).at[tuple(neighbour)].set(high)


def bell_draw(rng, extent, scale, limit, held_as=jnp.bfloat16):
    drawn = jax.random.normal(rng, extent, jnp.float32) * scale
    return jnp.minimum(jnp.maximum(drawn, -limit), limit).astype(held_as)


def setup_inputs(seed: int = 0) -> dict:
    splits = jax.random.split(jax.random.key(seed), 5)
    return {
        "series": draw_series(jax.random.fold_in(splits[4], 71), 0),
        "weights": plant(jax.random.randint(splits[1], (RUNS, FRAMES), 0, 3), jax.random.fold_in(splits[1], 1), 0, 2).astype(jnp.int32),
        "taps": bell_draw(splits[2], (2 * HALF + 1,), 0.3, 3.0),
        "lags": plant(jax.random.randint(splits[3], (COLS,), 0, LAGS), jax.random.fold_in(splits[3], 1), 0, LAGS - 1).astype(jnp.int32),
    }


epsilon = 1e-05

def filter_run(signal, taps, lags):
    padded = jnp.pad(signal.astype(jnp.float32), ((HALF, HALF + LAGS), (0, 0)))
    banded = jnp.zeros((FRAMES + LAGS, signal.shape[1]), jnp.float32)
    for tap_index in range(2 * HALF + 1):
        banded = banded + taps[tap_index].astype(jnp.float32) * padded[tap_index:tap_index + FRAMES + LAGS]
    shifted = jnp.zeros((FRAMES, signal.shape[1]), jnp.float32)
    for lag_value in range(LAGS):
        shifted = jnp.where(lags[None, :] == lag_value, banded[lag_value:lag_value + FRAMES], shifted)
    return shifted.astype(jnp.bfloat16)

def normalize(filtered, weight):
    values = filtered.astype(jnp.float32)
    total = jnp.sum(weight)
    first = lax.optimization_barrier(jnp.sum(weight[:, None] * values, axis=0)) / total
    second = lax.optimization_barrier(jnp.sum(weight[:, None] * values * values, axis=0)) / total
    scaling = lax.rsqrt(second - first * first + epsilon)
    scores = (jnp.sqrt(weight)[:, None] * (values - first) * scaling).astype(jnp.bfloat16)
    return (scores, total)

def reference(series, weights, taps, lags):
    positions = jnp.arange(ROWS, dtype=jnp.int32)
    seed_columns = positions % N_BLK * COL_DEV + positions // N_BLK * (COL_DEV // SEED_DEV)
    result = jnp.zeros((ROWS, COLS), jnp.float32)
    for run_index in range(RUNS):
        filtered = filter_run(series[run_index], taps, lags)
        scores, total = normalize(filtered, weights[run_index].astype(jnp.float32))
        seeds = jnp.take(scores, seed_columns, axis=1)
        result = result + jnp.dot(seeds.T, scores, preferred_element_type=jnp.float32) / total
    return result / RUNS
```

```python
import functools

import jax
import jax.numpy as jnp
from jax import lax
from jax.experimental import pallas as pl
from jax.experimental.pallas import tpu as pltpu
from jax.sharding import PartitionSpec as P

HALF = 16
LAGS = 4
SEED_DEV = 128
TAPS = 2 * HALF + 1
OUT_BLK = 224
IN_BLK = 256
CHUNK = 64
TOP = 32000.0
STEPS = 128.0
epsilon = 1e-05


def kernel(dims, x_ref, w_ref, taps_ref, lags_ref, out_ref, xrecv, xfull, toep, wcol, rcol, banded, filt,
           scores, seeds, stage, transit, final, own, ownrecv, xsem, dsend, fsend, srecv, tsend, trecv, frecv,
           osem):
    n_run, n_blk, frames, panel, fp, n_filter = dims
    half = panel // 2
    groups = half // 128
    total_frames = 2 * frames
    seeds_core = SEED_DEV // 2
    q_run = SEED_DEV // n_run
    rows_run = q_run * n_blk
    rows = rows_run // 2
    runs_core = n_run // 2

    z = lax.axis_index("run")
    tm = lax.axis_index("tm")
    blk = lax.axis_index("blk")
    other = 1 - tm

    def dev(run, core, block):
        return (run, core, block)

    barrier = pltpu.get_barrier_semaphore()
    mesh_id = pl.DeviceIdType.MESH
    pl.semaphore_signal(barrier, inc=1, device_id=dev(z, other, blk), device_id_type=mesh_id)
    for d in range(1, n_blk):
        peer = lax.rem(blk + d, n_blk)
        pl.semaphore_signal(barrier, inc=1, device_id=dev(z, tm, peer), device_id_type=mesh_id)

    @pl.when(z > 0)
    def _():
        for core in range(2):
            pl.semaphore_signal(barrier, inc=1, device_id=dev(z - 1, core, blk), device_id_type=mesh_id)

    @pl.when(z < n_run - 1)
    def _():
        for core in range(2):
            pl.semaphore_signal(barrier, inc=1, device_id=dev(z + 1, core, blk), device_id_type=mesh_id)

    inner = jnp.logical_and(z > 0, z < n_run - 1)
    pl.semaphore_wait(barrier, jnp.where(inner, n_blk + 4, n_blk + 2))

    mine = pl.ds(pl.multiple_of(tm * half, 128), half)
    theirs = pl.ds(pl.multiple_of(other * half, 128), half)
    swap = pltpu.make_async_remote_copy(
        src_ref=x_ref.at[:, theirs], dst_ref=xrecv, send_sem=xsem.at[0], recv_sem=xsem.at[1],
        device_id=dev(z, other, blk), device_id_type=mesh_id)
    swap.start()

    diff = (lax.broadcasted_iota(jnp.int32, (OUT_BLK, IN_BLK), 1)
            - lax.broadcasted_iota(jnp.int32, (OUT_BLK, IN_BLK), 0))
    band = jnp.zeros((OUT_BLK, IN_BLK), jnp.float32)
    for k in range(TAPS):
        band = jnp.where(diff == k, taps_ref[k], band)
    toep[...] = band.astype(jnp.bfloat16)

    wrow = w_ref[...].astype(jnp.float32)
    total = jnp.sum(wrow)
    wrow = jnp.concatenate([wrow, jnp.zeros((1, fp - total_frames), jnp.float32)], axis=1)
    for j in range(fp // 128):
        square = jnp.broadcast_to(wrow[:, j * 128:(j + 1) * 128], (128, 128)).T
        wcol[j * 128:(j + 1) * 128, :] = square
        rcol[j * 128:(j + 1) * 128, :] = jnp.sqrt(square)

    xfull[0:HALF, :] = jnp.zeros((HALF, half), jnp.float32)
    tail = HALF + total_frames
    xfull[tail:, :] = jnp.zeros((xfull.shape[0] - tail, half), jnp.float32)
    xfull[pl.ds(pl.multiple_of(HALF + tm * frames, 8), frames), :] = x_ref[:, mine].astype(jnp.float32)
    swap.wait_recv()
    xfull[pl.ds(pl.multiple_of(HALF + other * frames, 8), frames), :] = xrecv[...].astype(jnp.float32)

    for b in range(n_filter):
        banded[b * OUT_BLK:(b + 1) * OUT_BLK, :] = jnp.dot(
            toep[...], xfull[b * OUT_BLK:b * OUT_BLK + IN_BLK, :].astype(jnp.bfloat16),
            preferred_element_type=jnp.float32)

    lag_own = lags_ref[:, mine]
    for j in range(groups):
        lanes = slice(j * 128, (j + 1) * 128)
        lag = jnp.broadcast_to(lag_own[:, lanes], (CHUNK, 128))
        is_lag = [lag == v for v in range(LAGS)]

        def moments(i, carry, lanes=lanes, is_lag=is_lag):
            a1, a2 = carry
            r0 = pl.multiple_of(i * CHUNK, CHUNK)
            late = banded[pl.ds(r0, CHUNK + 8), lanes]
            v = late[0:CHUNK]
            for k in range(1, LAGS):
                v = jnp.where(is_lag[k], late[k:k + CHUNK], v)
            v = v.astype(jnp.bfloat16).astype(jnp.float32)
            filt[pl.ds(r0, CHUNK), lanes] = v
            wv = wcol[pl.ds(r0, CHUNK), :] * v
            a1 = a1 + jnp.sum(wv.reshape(CHUNK // 8, 8, 128), axis=0)
            a2 = a2 + jnp.sum((wv * v).reshape(CHUNK // 8, 8, 128), axis=0)
            return a1, a2

        zero = jnp.zeros((8, 128), jnp.float32)
        a1, a2 = lax.fori_loop(0, fp // CHUNK, moments, (zero, zero))
        first = jnp.sum(a1, axis=0, keepdims=True) / total
        second = jnp.sum(a2, axis=0, keepdims=True) / total
        scaling = lax.rsqrt(second - first * first + epsilon)

        def score(i, carry, lanes=lanes, first=first, scaling=scaling):
            r0 = pl.multiple_of(i * CHUNK, CHUNK)
            v = filt[pl.ds(r0, CHUNK), lanes]
            s = rcol[pl.ds(r0, CHUNK), :] * (v - first) * scaling
            scores[pl.ds(r0, CHUNK), lanes] = s.astype(jnp.bfloat16)
            return carry

        lax.fori_loop(0, fp // CHUNK, score, 0)

    pick = (lax.broadcasted_iota(jnp.int32, (seeds_core, half), 1)
            == (panel // SEED_DEV) * lax.broadcasted_iota(jnp.int32, (seeds_core, half), 0))
    seeds[blk, tm] = lax.dot_general(
        pick.astype(jnp.float32).astype(jnp.bfloat16), scores[...], (((1,), (1,)), ((), ())),
        preferred_element_type=jnp.float32).astype(jnp.bfloat16)

    def seed_copy(block, target, send):
        return pltpu.make_async_remote_copy(
            src_ref=seeds.at[block, tm], dst_ref=seeds.at[block, tm], send_sem=send,
            recv_sem=srecv.at[block, tm], device_id=target, device_id_type=mesh_id)

    for d in range(1, n_blk):
        peer = lax.rem(blk + d, n_blk)
        seed_copy(blk, dev(z, tm, peer), dsend.at[d]).start()
    seed_copy(blk, dev(z, other, blk), fsend.at[0]).start()
    for d in range(1, n_blk):
        peer = lax.rem(blk + n_blk - d, n_blk)
        pltpu.make_async_copy(seeds.at[peer, tm], seeds.at[peer, tm], srecv.at[peer, tm]).wait()
        seed_copy(peer, dev(z, other, blk), fsend.at[d]).start()
    for b in range(n_blk):
        pltpu.make_async_copy(seeds.at[b, other], seeds.at[b, other], srecv.at[b, other]).wait()

    i = lax.broadcasted_iota(jnp.int32, (rows_run, rows_run), 0)
    j = lax.broadcasted_iota(jnp.int32, (rows_run, rows_run), 1)
    n_vec = jnp.full((rows_run, rows_run), n_blk, jnp.int32)
    order = (j == lax.rem(i, n_vec) * q_run + lax.div(i, n_vec)).astype(jnp.float32).astype(jnp.bfloat16)

    def corr(r):
        core = lax.div(r, runs_core)
        q0 = pl.multiple_of(lax.rem(r, runs_core) * q_run, q_run)
        left = jnp.concatenate([seeds[b, core, pl.ds(q0, q_run), :] for b in range(n_blk)], axis=0)
        left = jnp.dot(order, left, preferred_element_type=jnp.float32).astype(jnp.bfloat16)
        return jnp.dot(left, scores[...], preferred_element_type=jnp.float32) / total

    code_row = groups * rows

    def encode(buf, v):
        peak = jnp.max(jnp.abs(v), axis=0, keepdims=True)
        lane = peak[:, 0:128]
        for g in range(1, groups):
            lane = jnp.maximum(lane, peak[:, g * 128:(g + 1) * 128])
        code = jnp.ceil(jnp.log2(jnp.maximum(lane, 1e-30)) * STEPS) + 1.0
        gain = TOP * jnp.exp2(code * (-1.0 / STEPS))
        for g in range(groups):
            scaled = jnp.round(v[:, g * 128:(g + 1) * 128] * gain)
            buf[g * rows:(g + 1) * rows, :] = scaled.astype(jnp.int32).astype(jnp.int16)
        buf[code_row:code_row + 16, :] = jnp.broadcast_to(code, (16, 128)).astype(jnp.int32).astype(jnp.int16)

    def decode(buf):
        code = buf[code_row:code_row + 16, :].astype(jnp.int32).astype(jnp.float32)[0:1, :]
        unit = jnp.exp2(code * (1.0 / STEPS)) * (1.0 / TOP)
        return jnp.concatenate(
            [buf[g * rows:(g + 1) * rows, :].astype(jnp.int32).astype(jnp.float32) * unit for g in range(groups)],
            axis=1)

    flip = (z >= runs_core).astype(jnp.int32)
    zz = z + flip * (n_run - 1 - 2 * z)

    def send_block(r, way, has_before):
        g = corr(r)
        nxt = z + 1 - 2 * way
        for h in range(2):
            own[h * rows:(h + 1) * rows, :] = g[h * rows:(h + 1) * rows, :]
        for h in range(2):

            @pl.when(has_before)
            def _():
                pltpu.make_async_copy(transit.at[r, h], transit.at[r, h], trecv.at[r, h]).wait()
                own[h * rows:(h + 1) * rows, :] += decode(transit.at[r, h])

            encode(stage.at[r, h], own[h * rows:(h + 1) * rows, :])

            @pl.when(r == nxt)
            def _():
                pltpu.make_async_remote_copy(
                    src_ref=stage.at[r, h], dst_ref=final.at[way, tm], send_sem=tsend.at[r, h],
                    recv_sem=frecv.at[way, tm], device_id=dev(nxt, h, blk), device_id_type=mesh_id).start()

            @pl.when(r != nxt)
            def _():
                pltpu.make_async_remote_copy(
                    src_ref=stage.at[r, h], dst_ref=transit.at[r, h], send_sem=tsend.at[r, h],
                    recv_sem=trecv.at[r, h], device_id=dev(nxt, tm, blk), device_id_type=mesh_id).start()

    def unflip(rr):
        return rr + flip * (n_run - 1 - 2 * rr)

    def step(k, carry):
        far = n_run - 1 - k

        @pl.when(far > zz)
        def _():
            send_block(unflip(far), flip, zz > 0)

        @pl.when(k < zz)
        def _():
            send_block(unflip(k), 1 - flip, zz < n_run - 1)

        return carry

    lax.fori_loop(0, n_run, step, 0)

    g = corr(z)
    own[...] = g
    keep = pl.ds(pl.multiple_of(tm * rows, rows), rows)
    give = pl.ds(pl.multiple_of(other * rows, rows), rows)
    trade = pltpu.make_async_remote_copy(
        src_ref=own.at[give, :], dst_ref=ownrecv, send_sem=osem.at[0], recv_sem=osem.at[1],
        device_id=dev(z, other, blk), device_id_type=mesh_id)
    trade.start()
    out_ref[:, mine] = own[keep, :]
    trade.wait_recv()
    out_ref[:, theirs] = ownrecv[...]
    for way, present in ((0, z > 0), (1, z < n_run - 1)):

        @pl.when(present)
        def _():
            for c in range(2):
                pltpu.make_async_copy(final.at[way, c], final.at[way, c], frecv.at[way, c]).wait()
                cols = slice(c * half, (c + 1) * half)
                out_ref[:, cols] += decode(final.at[way, c])

    out_ref[...] = out_ref[...] / n_run

    swap.wait_send()
    trade.wait_send()
    for d in range(n_blk):
        if d:
            seed_copy(blk, dev(z, tm, lax.rem(blk + d, n_blk)), dsend.at[d]).wait_send()
        seed_copy(blk, dev(z, other, blk), fsend.at[d]).wait_send()

    def drain(r, carry):
        @pl.when(r != z)
        def _():
            for h in range(2):
                pltpu.make_async_remote_copy(
                    src_ref=stage.at[r, h], dst_ref=transit.at[r, h], send_sem=tsend.at[r, h],
                    recv_sem=trecv.at[r, h], device_id=dev(z, other, blk), device_id_type=mesh_id).wait_send()

        return carry

    lax.fori_loop(0, n_run, drain, 0)


def local(n_run, n_blk, series, weights, taps, lags):
    signal = series[0]
    frames, panel = signal.shape
    half = panel // 2
    fp = -(-2 * frames // 256) * 256
    n_filter = -(-(fp + LAGS) // OUT_BLK)
    rows_run = SEED_DEV // n_run * n_blk
    rows = rows_run // 2
    message = (half // 128) * rows + 16
    vmem = pl.BlockSpec(memory_space=pltpu.VMEM)
    dma = pltpu.SemaphoreType.DMA
    f32, b16 = jnp.float32, jnp.bfloat16
    flops = 2 * half * fp * (IN_BLK + n_blk * SEED_DEV)
    return pl.pallas_call(
        functools.partial(kernel, (n_run, n_blk, frames, panel, fp, n_filter)),
        out_shape=jax.ShapeDtypeStruct((rows, panel), f32),
        in_specs=[vmem, vmem, pl.BlockSpec(memory_space=pltpu.SMEM), vmem],
        out_specs=vmem,
        scratch_shapes=[
            pltpu.VMEM((frames, half), b16),
            pltpu.VMEM((n_filter * OUT_BLK + IN_BLK - OUT_BLK, half), f32),
            pltpu.VMEM((OUT_BLK, IN_BLK), b16),
            pltpu.VMEM((fp, 128), f32),
            pltpu.VMEM((fp, 128), f32),
            pltpu.VMEM((n_filter * OUT_BLK, half), f32),
            pltpu.VMEM((fp, half), f32),
            pltpu.VMEM((fp, half), b16),
            pltpu.VMEM((n_blk, 2, SEED_DEV // 2, fp), b16),
            pltpu.VMEM((n_run, 2, message, 128), jnp.int16),
            pltpu.VMEM((n_run, 2, message, 128), jnp.int16),
            pltpu.VMEM((2, 2, message, 128), jnp.int16),
            pltpu.VMEM((rows_run, half), f32),
            pltpu.VMEM((rows, half), f32),
            dma((2,)),
            dma((n_blk,)),
            dma((n_blk,)),
            dma((n_blk, 2)),
            dma((n_run, 2)),
            dma((n_run, 2)),
            dma((2, 2)),
            dma((2,)),
        ],
        compiler_params=pltpu.CompilerParams(
            collective_id=0, has_side_effects=True, vmem_limit_bytes=56 * 1024 * 1024),
        cost_estimate=pl.CostEstimate(flops=flops, bytes_accessed=2 * frames * panel, transcendentals=0),
    )(signal, weights, taps.astype(f32), lags[None, :])


def solution(mesh):
    placed = (P("run", "tm", "blk"), P("run", None), P(), P("blk"))
    body = functools.partial(local, mesh.shape["run"], mesh.shape["blk"])
    return jax.shard_map(
        body, mesh=mesh, in_specs=placed, out_specs=P(("run", "tm"), "blk"), check_vma=False
    )
```

```python
import functools

import jax
import jax.numpy as jnp
from jax import lax
from jax.experimental import pallas as pl
from jax.experimental.pallas import tpu as pltpu
from jax.sharding import PartitionSpec as P

HALF = 16
LAGS = 4
SEED_DEV = 128
TAPS = 2 * HALF + 1
OUT_BLK = 224
IN_BLK = 256
CHUNK = 128
TOP = 32000.0
STEPS = 128.0
epsilon = 1e-05


def kernel(dims, x_ref, w_ref, taps_ref, lags_ref, out_ref, sown, sother, sfull, sscore, xrecv, xfull, toep, wcol,
           rcol, lagscr, banded, filt, scores, seeds, stage, transit, final, own, ownrecv, xsem, dsend, srecv, tsend,
           trecv, frecv, osem):
    n_run, n_blk, frames, panel, fp, n_filter = dims
    half = panel // 2
    groups = half // 128
    total_frames = 2 * frames
    q_run = SEED_DEV // n_run
    rows_run = q_run * n_blk
    rows = rows_run // 2
    runs_core = n_run // 2

    z = lax.axis_index("run")
    tm = lax.axis_index("tm")
    blk = lax.axis_index("blk")
    other = 1 - tm

    def dev(run, core, block):
        return (run, core, block)

    barrier = pltpu.get_barrier_semaphore()
    mesh_id = pl.DeviceIdType.MESH
    pl.semaphore_signal(barrier, inc=1, device_id=dev(z, other, blk), device_id_type=mesh_id)
    for d in range(1, n_blk):
        peer = lax.rem(blk + d, n_blk)
        pl.semaphore_signal(barrier, inc=1, device_id=dev(z, tm, peer), device_id_type=mesh_id)

    @pl.when(z > 0)
    def _():
        for core in range(2):
            pl.semaphore_signal(barrier, inc=1, device_id=dev(z - 1, core, blk), device_id_type=mesh_id)

    @pl.when(z < n_run - 1)
    def _():
        for core in range(2):
            pl.semaphore_signal(barrier, inc=1, device_id=dev(z + 1, core, blk), device_id_type=mesh_id)

    def one_hot(mask):
        return mask.astype(jnp.float32).astype(jnp.bfloat16)

    pick = one_hot(lax.broadcasted_iota(jnp.int32, (panel, SEED_DEV), 0)
                   == (panel // SEED_DEV) * lax.broadcasted_iota(jnp.int32, (panel, SEED_DEV), 1))
    sown[...] = jnp.dot(x_ref[...], pick, preferred_element_type=jnp.float32).astype(jnp.bfloat16)

    inner = jnp.logical_and(z > 0, z < n_run - 1)
    pl.semaphore_wait(barrier, jnp.where(inner, n_blk + 4, n_blk + 2))

    mine = pl.ds(pl.multiple_of(tm * half, 128), half)
    theirs = pl.ds(pl.multiple_of(other * half, 128), half)
    sswap = pltpu.make_async_remote_copy(
        src_ref=sown, dst_ref=sother, send_sem=xsem.at[2], recv_sem=xsem.at[3],
        device_id=dev(z, other, blk), device_id_type=mesh_id)
    sswap.start()
    swap = pltpu.make_async_remote_copy(
        src_ref=x_ref.at[:, theirs], dst_ref=xrecv, send_sem=xsem.at[0], recv_sem=xsem.at[1],
        device_id=dev(z, other, blk), device_id_type=mesh_id)
    swap.start()

    diff = (lax.broadcasted_iota(jnp.int32, (OUT_BLK, IN_BLK), 1)
            - lax.broadcasted_iota(jnp.int32, (OUT_BLK, IN_BLK), 0))
    band = jnp.zeros((OUT_BLK, IN_BLK), jnp.float32)
    for k in range(TAPS):
        band = jnp.where(diff == k, taps_ref[k], band)
    toep[...] = band.astype(jnp.bfloat16)

    wrow = w_ref[...].astype(jnp.float32)
    total = jnp.sum(wrow)
    wrow = jnp.concatenate([wrow, jnp.zeros((1, fp - total_frames), jnp.float32)], axis=1)
    for j in range(fp // 128):
        square = jnp.broadcast_to(wrow[:, j * 128:(j + 1) * 128], (128, 128)).T
        wcol[j * 128:(j + 1) * 128, :] = square
        rcol[j * 128:(j + 1) * 128, :] = jnp.sqrt(square)

    tail = HALF + total_frames
    near = pl.ds(pl.multiple_of(HALF + tm * frames, 8), frames)
    far_rows = pl.ds(pl.multiple_of(HALF + other * frames, 8), frames)

    def edges(ref, width):
        ref[0:HALF, :] = jnp.zeros((HALF, width), jnp.float32)
        ref[tail:, :] = jnp.zeros((ref.shape[0] - tail, width), jnp.float32)

    def normalize(src, lanes, lag, dst):
        width = lag.shape[1]
        for b in range(n_filter):
            banded[b * OUT_BLK:(b + 1) * OUT_BLK, 0:width] = jnp.dot(
                toep[...], src[b * OUT_BLK:b * OUT_BLK + IN_BLK, lanes].astype(jnp.bfloat16),
                preferred_element_type=jnp.float32)
        for g in range(width // 128):
            part = slice(g * 128, (g + 1) * 128)
            odd = jnp.broadcast_to((lag[:, part] & 1) == 1, (CHUNK + 8, 128))
            high = jnp.broadcast_to(lag[:, part] >= 2, (CHUNK, 128))
            sums = []
            for r0 in range(0, fp, CHUNK):
                late = banded[r0:r0 + CHUNK + 16, part]
                v = jnp.where(odd, late[1:CHUNK + 9], late[0:CHUNK + 8])
                v = jnp.where(high, v[2:CHUNK + 2], v[0:CHUNK])
                v = v.astype(jnp.bfloat16).astype(jnp.float32)
                filt[r0:r0 + CHUNK, part] = v
                wv = wcol[r0:r0 + CHUNK, :] * v
                sums.append((jnp.sum(wv.reshape(CHUNK // 8, 8, 128), axis=0),
                             jnp.sum((wv * v).reshape(CHUNK // 8, 8, 128), axis=0)))
            first = jnp.sum(sum(a for a, _ in sums), axis=0, keepdims=True) / total
            second = jnp.sum(sum(a for _, a in sums), axis=0, keepdims=True) / total
            scaling = lax.rsqrt(second - first * first + epsilon)
            for r0 in range(0, fp, CHUNK):
                v = rcol[r0:r0 + CHUNK, :] * (filt[r0:r0 + CHUNK, part] - first) * scaling
                dst(r0, g, v.astype(jnp.bfloat16))

    edges(sfull, SEED_DEV)
    sfull[near, :] = sown[...].astype(jnp.float32)
    lag_rows = [lags_ref[j:j + 1, :] for j in range(panel // 128)]
    lag_all = jnp.broadcast_to(jnp.concatenate(lag_rows, axis=1), (8, panel)).astype(jnp.float32)
    seed_lag = jnp.dot(lag_all.astype(jnp.bfloat16), pick, preferred_element_type=jnp.float32)
    seed_lag = seed_lag.astype(jnp.int32)[0:1, :]
    sswap.wait_recv()
    sfull[far_rows, :] = sother[...].astype(jnp.float32)

    def seed_store(r0, g, v):
        sscore[r0:r0 + CHUNK, :] = v

    normalize(sfull, slice(0, SEED_DEV), seed_lag, seed_store)
    eye = one_hot(lax.broadcasted_iota(jnp.int32, (SEED_DEV, SEED_DEV), 1)
                  == lax.broadcasted_iota(jnp.int32, (SEED_DEV, SEED_DEV), 0))
    rows_seed = lax.dot_general(
        eye, sscore[...], (((1,), (1,)), ((), ())), preferred_element_type=jnp.float32).astype(jnp.bfloat16)
    for r in range(n_run):
        seeds[blk, r] = rows_seed[r * q_run:(r + 1) * q_run, :]

    flip = (z >= runs_core).astype(jnp.int32)
    zz = z + flip * (n_run - 1 - 2 * z)

    def unflip(rr):
        return rr + flip * (n_run - 1 - 2 * rr)

    def in_order(away, back):
        def step(k, carry):
            far = n_run - 1 - k

            @pl.when(far > zz)
            def _():
                away(unflip(far))

            @pl.when(k < zz)
            def _():
                back(unflip(k))

            return carry

        lax.fori_loop(0, n_run, step, 0)

    def seed_copy(d, r):
        return pltpu.make_async_remote_copy(
            src_ref=seeds.at[blk, r], dst_ref=seeds.at[blk, r], send_sem=dsend.at[d, r],
            recv_sem=srecv.at[blk, r], device_id=dev(z, tm, lax.rem(blk + d, n_blk)), device_id_type=mesh_id)

    def send_seeds(r):
        for d in range(1, n_blk):
            seed_copy(d, r).start()

    in_order(send_seeds, send_seeds)
    send_seeds(z)

    edges(xfull, half)
    xfull[near, :] = x_ref[:, mine].astype(jnp.float32)
    swap.wait_recv()
    xfull[far_rows, :] = xrecv[...].astype(jnp.float32)
    lag_own = jnp.where(tm == 0, jnp.concatenate(lag_rows[:groups], axis=1),
                        jnp.concatenate(lag_rows[groups:], axis=1))
    for g in range(groups):
        lagscr[g:g + 1, :] = lag_own[:, g * 128:(g + 1) * 128]

    def pair(p, carry):
        lane0 = pl.multiple_of(p * 256, 256)
        lag = jnp.concatenate([lagscr[pl.ds(2 * p, 1), :], lagscr[pl.ds(2 * p + 1, 1), :]], axis=1)

        def store(r0, g, v):
            scores[r0:r0 + CHUNK, pl.ds(pl.multiple_of(lane0 + g * 128, 128), 128)] = v

        normalize(xfull, pl.ds(lane0, 256), lag, store)
        return carry

    lax.fori_loop(0, half // 256, pair, 0)

    i = lax.broadcasted_iota(jnp.int32, (rows_run, rows_run), 0)
    j = lax.broadcasted_iota(jnp.int32, (rows_run, rows_run), 1)
    n_vec = jnp.full((rows_run, rows_run), n_blk, jnp.int32)
    order = one_hot(j == lax.rem(i, n_vec) * q_run + lax.div(i, n_vec))

    def corr(r):
        for d in range(1, n_blk):
            peer = lax.rem(blk + d, n_blk)
            pltpu.make_async_copy(seeds.at[peer, r], seeds.at[peer, r], srecv.at[peer, r]).wait()
        left = jnp.concatenate([seeds[b, r] for b in range(n_blk)], axis=0)
        left = jnp.dot(order, left, preferred_element_type=jnp.float32).astype(jnp.bfloat16)
        return jnp.dot(left, scores[...], preferred_element_type=jnp.float32) / total

    code_row = groups * rows

    def encode(buf, v):
        peak = jnp.max(jnp.abs(v), axis=0, keepdims=True)
        lane = peak[:, 0:128]
        for g in range(1, groups):
            lane = jnp.maximum(lane, peak[:, g * 128:(g + 1) * 128])
        code = jnp.ceil(jnp.log2(jnp.maximum(lane, 1e-30)) * STEPS) + 1.0
        gain = TOP * jnp.exp2(code * (-1.0 / STEPS))
        for g in range(groups):
            scaled = jnp.round(v[:, g * 128:(g + 1) * 128] * gain)
            buf[g * rows:(g + 1) * rows, :] = scaled.astype(jnp.int32).astype(jnp.int16)
        buf[code_row:code_row + 16, :] = jnp.broadcast_to(code, (16, 128)).astype(jnp.int32).astype(jnp.int16)

    def decode(buf):
        code = buf[code_row:code_row + 16, :].astype(jnp.int32).astype(jnp.float32)[0:1, :]
        unit = jnp.exp2(code * (1.0 / STEPS)) * (1.0 / TOP)
        return jnp.concatenate(
            [buf[g * rows:(g + 1) * rows, :].astype(jnp.int32).astype(jnp.float32) * unit for g in range(groups)],
            axis=1)

    def send_block(r, way, has_before):
        g = corr(r)
        nxt = z + 1 - 2 * way
        for h in range(2):
            own[h * rows:(h + 1) * rows, :] = g[h * rows:(h + 1) * rows, :]
        for h in range(2):

            @pl.when(has_before)
            def _():
                pltpu.make_async_copy(transit.at[r, h], transit.at[r, h], trecv.at[r, h]).wait()
                own[h * rows:(h + 1) * rows, :] += decode(transit.at[r, h])

            encode(stage.at[r, h], own[h * rows:(h + 1) * rows, :])

            @pl.when(r == nxt)
            def _():
                pltpu.make_async_remote_copy(
                    src_ref=stage.at[r, h], dst_ref=final.at[way, tm], send_sem=tsend.at[r, h],
                    recv_sem=frecv.at[way, tm], device_id=dev(nxt, h, blk), device_id_type=mesh_id).start()

            @pl.when(r != nxt)
            def _():
                pltpu.make_async_remote_copy(
                    src_ref=stage.at[r, h], dst_ref=transit.at[r, h], send_sem=tsend.at[r, h],
                    recv_sem=trecv.at[r, h], device_id=dev(nxt, tm, blk), device_id_type=mesh_id).start()

    in_order(lambda r: send_block(r, flip, zz > 0), lambda r: send_block(r, 1 - flip, zz < n_run - 1))

    g = corr(z)
    own[...] = g
    keep = pl.ds(pl.multiple_of(tm * rows, rows), rows)
    give = pl.ds(pl.multiple_of(other * rows, rows), rows)
    trade = pltpu.make_async_remote_copy(
        src_ref=own.at[give, :], dst_ref=ownrecv, send_sem=osem.at[0], recv_sem=osem.at[1],
        device_id=dev(z, other, blk), device_id_type=mesh_id)
    trade.start()
    out_ref[:, mine] = own[keep, :]
    trade.wait_recv()
    out_ref[:, theirs] = ownrecv[...]
    for way, present in ((0, z > 0), (1, z < n_run - 1)):

        @pl.when(present)
        def _():
            for c in range(2):
                pltpu.make_async_copy(final.at[way, c], final.at[way, c], frecv.at[way, c]).wait()
                cols = slice(c * half, (c + 1) * half)
                out_ref[:, cols] += decode(final.at[way, c])

    out_ref[...] = out_ref[...] / n_run

    sswap.wait_send()
    swap.wait_send()
    trade.wait_send()

    def drain(r, carry):
        for d in range(1, n_blk):
            seed_copy(d, r).wait_send()

        @pl.when(r != z)
        def _():
            for h in range(2):
                pltpu.make_async_remote_copy(
                    src_ref=stage.at[r, h], dst_ref=transit.at[r, h], send_sem=tsend.at[r, h],
                    recv_sem=trecv.at[r, h], device_id=dev(z, other, blk), device_id_type=mesh_id).wait_send()

        return carry

    lax.fori_loop(0, n_run, drain, 0)


def local(n_run, n_blk, series, weights, taps, lags):
    signal = series[0]
    frames, panel = signal.shape
    half = panel // 2
    fp = -(-2 * frames // 256) * 256
    n_filter = -(-(fp + LAGS) // OUT_BLK)
    rows_run = SEED_DEV // n_run * n_blk
    rows = rows_run // 2
    message = (half // 128) * rows + 16
    vmem = pl.BlockSpec(memory_space=pltpu.VMEM)
    dma = pltpu.SemaphoreType.DMA
    f32, b16 = jnp.float32, jnp.bfloat16
    flops = 2 * half * fp * (IN_BLK + n_blk * SEED_DEV)
    return pl.pallas_call(
        functools.partial(kernel, (n_run, n_blk, frames, panel, fp, n_filter)),
        out_shape=jax.ShapeDtypeStruct((rows, panel), f32),
        in_specs=[vmem, vmem, pl.BlockSpec(memory_space=pltpu.SMEM), vmem],
        out_specs=vmem,
        scratch_shapes=[
            pltpu.VMEM((frames, SEED_DEV), b16),
            pltpu.VMEM((frames, SEED_DEV), b16),
            pltpu.VMEM((n_filter * OUT_BLK + IN_BLK - OUT_BLK, SEED_DEV), f32),
            pltpu.VMEM((fp, SEED_DEV), b16),
            pltpu.VMEM((frames, half), b16),
            pltpu.VMEM((n_filter * OUT_BLK + IN_BLK - OUT_BLK, half), f32),
            pltpu.VMEM((OUT_BLK, IN_BLK), b16),
            pltpu.VMEM((fp, 128), f32),
            pltpu.VMEM((fp, 128), f32),
            pltpu.VMEM((half // 128, 128), jnp.int32),
            pltpu.VMEM((n_filter * OUT_BLK, 256), f32),
            pltpu.VMEM((fp, 256), f32),
            pltpu.VMEM((fp, half), b16),
            pltpu.VMEM((n_blk, n_run, SEED_DEV // n_run, fp), b16),
            pltpu.VMEM((n_run, 2, message, 128), jnp.int16),
            pltpu.VMEM((n_run, 2, message, 128), jnp.int16),
            pltpu.VMEM((2, 2, message, 128), jnp.int16),
            pltpu.VMEM((rows_run, half), f32),
            pltpu.VMEM((rows, half), f32),
            dma((4,)),
            dma((n_blk, n_run)),
            dma((n_blk, n_run)),
            dma((n_run, 2)),
            dma((n_run, 2)),
            dma((2, 2)),
            dma((2,)),
        ],
        compiler_params=pltpu.CompilerParams(
            collective_id=0, has_side_effects=True, vmem_limit_bytes=56 * 1024 * 1024),
        cost_estimate=pl.CostEstimate(flops=flops, bytes_accessed=2 * frames * panel, transcendentals=0),
    )(signal, weights, taps.astype(f32), lags.reshape(panel // 128, 128))


def solution(mesh):
    placed = (P("run", "tm", "blk"), P("run", None), P(), P("blk"))
    body = functools.partial(local, mesh.shape["run"], mesh.shape["blk"])
    return jax.shard_map(
        body, mesh=mesh, in_specs=placed, out_specs=P(("run", "tm"), "blk"), check_vma=False
    )
```

```python
import functools

import jax
import jax.numpy as jnp
from jax import lax
from jax.experimental import pallas as pl
from jax.experimental.pallas import tpu as pltpu
from jax.sharding import PartitionSpec as P

HALF = 16
LAGS = 4
SEED_DEV = 128
TAPS = 2 * HALF + 1
OUT_BLK = 224
IN_BLK = 256
CHUNK = 128
WIDE = 256
TOP = 32000.0
STEPS = 128.0
epsilon = 1e-05


def kernel(dims, x_hbm, w_ref, taps_ref, lags_ref, out_ref, x_ref, sown, sother, sfull, sscore, xrecv, xfull, toep, wcol,
           rcol, lagscr, banded, filt, scores, seeds, left, stage, transit, final, part, own, ownrecv, xsem, dsend, srecv, tsend,
           trecv, frecv, osem):
    n_run, n_blk, frames, panel, fp, n_filter = dims
    half = panel // 2
    groups = half // 128
    total_frames = 2 * frames
    q_run = SEED_DEV // n_run
    rows_run = q_run * n_blk
    rows = rows_run // 2
    runs_core = n_run // 2

    z = lax.axis_index("run")
    tm = lax.axis_index("tm")
    blk = lax.axis_index("blk")
    other = 1 - tm

    def dev(run, core, block):
        return (run, core, block)

    barrier = pltpu.get_barrier_semaphore()
    mesh_id = pl.DeviceIdType.MESH
    pl.semaphore_signal(barrier, inc=1, device_id=dev(z, other, blk), device_id_type=mesh_id)
    for d in range(1, n_blk):
        peer = lax.rem(blk + d, n_blk)
        pl.semaphore_signal(barrier, inc=1, device_id=dev(z, tm, peer), device_id_type=mesh_id)

    @pl.when(z > 0)
    def _():
        for core in range(2):
            pl.semaphore_signal(barrier, inc=1, device_id=dev(z - 1, core, blk), device_id_type=mesh_id)

    @pl.when(z < n_run - 1)
    def _():
        for core in range(2):
            pl.semaphore_signal(barrier, inc=1, device_id=dev(z + 1, core, blk), device_id_type=mesh_id)

    mine = pl.ds(pl.multiple_of(tm * half, 128), half)
    theirs = pl.ds(pl.multiple_of(other * half, 128), half)
    load = pltpu.make_async_copy(x_hbm, x_ref, xsem.at[4])
    load.start()

    diff = (lax.broadcasted_iota(jnp.int32, (OUT_BLK, IN_BLK), 1)
            - lax.broadcasted_iota(jnp.int32, (OUT_BLK, IN_BLK), 0))
    band = jnp.zeros((OUT_BLK, IN_BLK), jnp.float32)
    for k in range(TAPS):
        band = jnp.where(diff == k, taps_ref[k].astype(jnp.float32), band)
    toep[...] = band.astype(jnp.bfloat16)

    wrow = w_ref[...].astype(jnp.float32)
    total = jnp.sum(wrow)
    wrow = jnp.concatenate([wrow, jnp.zeros((1, fp - total_frames), jnp.float32)], axis=1)
    for j in range(fp // 128):
        square = jnp.broadcast_to(wrow[:, j * 128:(j + 1) * 128], (128, 128)).T
        wcol[j * 128:(j + 1) * 128, :] = square
        rcol[j * 128:(j + 1) * 128, :] = jnp.sqrt(square)

    def one_hot(mask):
        return mask.astype(jnp.float32).astype(jnp.bfloat16)

    pick = one_hot(lax.broadcasted_iota(jnp.int32, (panel, SEED_DEV), 0)
                   == (panel // SEED_DEV) * lax.broadcasted_iota(jnp.int32, (panel, SEED_DEV), 1))
    load.wait()
    sown[...] = jnp.dot(x_ref[...], pick, preferred_element_type=jnp.float32).astype(jnp.bfloat16)

    inner = jnp.logical_and(z > 0, z < n_run - 1)
    pl.semaphore_wait(barrier, jnp.where(inner, n_blk + 4, n_blk + 2))

    sswap = pltpu.make_async_remote_copy(
        src_ref=sown, dst_ref=sother, send_sem=xsem.at[2], recv_sem=xsem.at[3],
        device_id=dev(z, other, blk), device_id_type=mesh_id)
    sswap.start()
    swap = pltpu.make_async_remote_copy(
        src_ref=x_ref.at[:, theirs], dst_ref=xrecv, send_sem=xsem.at[0], recv_sem=xsem.at[1],
        device_id=dev(z, other, blk), device_id_type=mesh_id)
    swap.start()

    tail = HALF + total_frames
    near = pl.ds(pl.multiple_of(HALF + tm * frames, 8), frames)
    far_rows = pl.ds(pl.multiple_of(HALF + other * frames, 8), frames)

    def edges(ref, width):
        ref[0:HALF, :] = jnp.zeros((HALF, width), jnp.float32)
        ref[tail:, :] = jnp.zeros((ref.shape[0] - tail, width), jnp.float32)

    def normalize(src, lanes, lag, dst):
        width = lag.shape[1]
        for b in range(n_filter):
            banded[b * OUT_BLK:(b + 1) * OUT_BLK, 0:width] = jnp.dot(
                toep[...], src[b * OUT_BLK:b * OUT_BLK + IN_BLK, lanes].astype(jnp.bfloat16),
                preferred_element_type=jnp.float32)
        for g in range(width // 128):
            part = slice(g * 128, (g + 1) * 128)
            odd = jnp.broadcast_to((lag[:, part] & 1) == 1, (CHUNK + 8, 128))
            high = jnp.broadcast_to(lag[:, part] >= 2, (CHUNK, 128))
            sums = []
            for r0 in range(0, fp, CHUNK):
                late = banded[r0:r0 + CHUNK + 16, part]
                v = jnp.where(odd, late[1:CHUNK + 9], late[0:CHUNK + 8])
                v = jnp.where(high, v[2:CHUNK + 2], v[0:CHUNK])
                v = v.astype(jnp.bfloat16).astype(jnp.float32)
                filt[r0:r0 + CHUNK, part] = v
                wv = wcol[r0:r0 + CHUNK, :] * v
                sums.append((jnp.sum(wv.reshape(CHUNK // 8, 8, 128), axis=0),
                             jnp.sum((wv * v).reshape(CHUNK // 8, 8, 128), axis=0)))
            first = jnp.sum(sum(a for a, _ in sums), axis=0, keepdims=True) / total
            second = jnp.sum(sum(a for _, a in sums), axis=0, keepdims=True) / total
            scaling = lax.rsqrt(second - first * first + epsilon)
            for r0 in range(0, fp, CHUNK):
                v = rcol[r0:r0 + CHUNK, :] * (filt[r0:r0 + CHUNK, part] - first) * scaling
                dst(r0, g, v.astype(jnp.bfloat16))

    edges(sfull, SEED_DEV)
    sfull[near, :] = sown[...].astype(jnp.float32)
    lag_rows = [lags_ref[j:j + 1, :] for j in range(panel // 128)]
    lag_all = jnp.broadcast_to(jnp.concatenate(lag_rows, axis=1), (8, panel)).astype(jnp.float32)
    seed_lag = jnp.dot(lag_all.astype(jnp.bfloat16), pick, preferred_element_type=jnp.float32)
    seed_lag = seed_lag.astype(jnp.int32)[0:1, :]
    edges(xfull, half)
    xfull[near, :] = x_ref[:, mine].astype(jnp.float32)
    sswap.wait_recv()
    sfull[far_rows, :] = sother[...].astype(jnp.float32)

    def seed_store(r0, g, v):
        sscore[r0:r0 + CHUNK, :] = v

    normalize(sfull, slice(0, SEED_DEV), seed_lag, seed_store)
    eye = one_hot(lax.broadcasted_iota(jnp.int32, (SEED_DEV, SEED_DEV), 1)
                  == lax.broadcasted_iota(jnp.int32, (SEED_DEV, SEED_DEV), 0))
    rows_seed = lax.dot_general(
        eye, sscore[...], (((1,), (1,)), ((), ())), preferred_element_type=jnp.float32).astype(jnp.bfloat16)
    for r in range(n_run):
        seeds[blk, r] = rows_seed[r * q_run:(r + 1) * q_run, :]

    flip = (z >= runs_core).astype(jnp.int32)
    zz = z + flip * (n_run - 1 - 2 * z)

    def unflip(rr):
        return rr + flip * (n_run - 1 - 2 * rr)

    def in_order(out, home, skip=False):
        def step(k, carry):
            far = n_run - 1 - k

            @pl.when(jnp.logical_and(far > zz, k > 0) if skip else far > zz)
            def _():
                out(unflip(far))

            @pl.when(k < zz)
            def _():
                home(unflip(k))

            return carry

        lax.fori_loop(0, n_run, step, 0)

    def seed_copy(d, r):
        return pltpu.make_async_remote_copy(
            src_ref=seeds.at[blk, r], dst_ref=seeds.at[blk, r], send_sem=dsend.at[d, r],
            recv_sem=srecv.at[blk, r], device_id=dev(z, tm, lax.rem(blk + d, n_blk)), device_id_type=mesh_id)

    def send_seeds(r):
        for d in range(1, n_blk):
            seed_copy(d, r).start()

    in_order(send_seeds, send_seeds)
    send_seeds(z)

    swap.wait_recv()
    xfull[far_rows, :] = xrecv[...].astype(jnp.float32)
    lag_own = jnp.where(tm == 0, jnp.concatenate(lag_rows[:groups], axis=1),
                        jnp.concatenate(lag_rows[groups:], axis=1))
    for g in range(groups):
        lagscr[g:g + 1, :] = lag_own[:, g * 128:(g + 1) * 128]

    i = lax.broadcasted_iota(jnp.int32, (rows_run, rows_run), 0)
    j = lax.broadcasted_iota(jnp.int32, (rows_run, rows_run), 1)
    n_vec = jnp.full((rows_run, rows_run), n_blk, jnp.int32)
    order = one_hot(j == lax.rem(i, n_vec) * q_run + lax.div(i, n_vec))

    def prepare(r):
        for d in range(1, n_blk):
            peer = lax.rem(blk + d, n_blk)
            pltpu.make_async_copy(seeds.at[peer, r], seeds.at[peer, r], srecv.at[peer, r]).wait()
        rows_left = jnp.concatenate([seeds[b, r] for b in range(n_blk)], axis=0)
        left[...] = jnp.dot(order, rows_left, preferred_element_type=jnp.float32).astype(jnp.bfloat16)

    def corr(p):
        cols = pl.ds(pl.multiple_of(p * WIDE, WIDE), WIDE)
        return jnp.dot(left[...], scores[:, cols], preferred_element_type=jnp.float32) / total

    def encode(buf, at, v):
        count = v.shape[0]
        peak = jnp.max(jnp.abs(v), axis=0, keepdims=True)
        lane = jnp.maximum(peak[:, 0:128], peak[:, 128:256])
        code = jnp.ceil(jnp.log2(jnp.maximum(lane, 1e-30)) * STEPS) + 1.0
        gain = TOP * jnp.exp2(code * (-1.0 / STEPS))
        for g in range(2):
            scaled = jnp.round(v[:, g * 128:(g + 1) * 128] * gain)
            buf[at + g * count:at + (g + 1) * count, :] = scaled.astype(jnp.int32).astype(jnp.int16)
        at += 2 * count
        buf[at:at + 16, :] = jnp.broadcast_to(code, (16, 128)).astype(jnp.int32).astype(jnp.int16)

    def decode(buf, count):
        code = buf[2 * count:2 * count + 16, :].astype(jnp.int32).astype(jnp.float32)[0:1, :]
        unit = jnp.exp2(code * (1.0 / STEPS)) * (1.0 / TOP)
        return jnp.concatenate(
            [buf[g * count:(g + 1) * count, :].astype(jnp.int32).astype(jnp.float32) * unit for g in range(2)],
            axis=1)

    long, short = 2 * rows_run + 16, 2 * rows + 16

    def pass_on(r, p):
        nxt = jnp.where(r > z, z + 1, z - 1)
        return pltpu.make_async_remote_copy(
            src_ref=stage.at[r, p, pl.ds(0, long)], dst_ref=transit.at[r, p], send_sem=tsend.at[r, p, 0],
            recv_sem=trecv.at[r, p], device_id=dev(nxt, tm, blk), device_id_type=mesh_id)

    def deliver(r, p, h):
        way = jnp.where(r > z, 0, 1)
        return pltpu.make_async_remote_copy(
            src_ref=stage.at[r, p, pl.ds(h * short, short)], dst_ref=final.at[way, tm, p],
            send_sem=tsend.at[r, p, h], recv_sem=frecv.at[way, tm, p],
            device_id=dev(r, h, blk), device_id_type=mesh_id)

    def send_block(r, way, has_before, p):
        nxt = z + 1 - 2 * way
        part[...] = corr(p)

        @pl.when(has_before)
        def _():
            pltpu.make_async_copy(transit.at[r, p], transit.at[r, p], trecv.at[r, p]).wait()
            part[...] += decode(transit.at[r, p], rows_run)

        @pl.when(r == nxt)
        def _():
            for h in range(2):
                encode(stage.at[r, p], h * short, part[h * rows:(h + 1) * rows, :])
                deliver(r, p, h).start()

        @pl.when(r != nxt)
        def _():
            encode(stage.at[r, p], 0, part[...])
            pass_on(r, p).start()

    def away(r, p):
        send_block(r, flip, zz > 0, p)

    def back(r, p):
        send_block(r, 1 - flip, zz < n_run - 1, p)

    n_wide = half // WIDE
    farthest = unflip(n_run - 1)
    late = (zz > 0).astype(jnp.int32)

    def pair(p, carry):
        @pl.when(p < n_wide)
        def _():
            lane0 = pl.multiple_of(p * WIDE, WIDE)
            lag = jnp.concatenate([lagscr[pl.ds(2 * p, 1), :], lagscr[pl.ds(2 * p + 1, 1), :]], axis=1)

            def store(r0, g, v):
                scores[r0:r0 + CHUNK, pl.ds(pl.multiple_of(lane0 + g * 128, 128), 128)] = v

            normalize(xfull, pl.ds(lane0, WIDE), lag, store)

        t = p - late

        @pl.when(t == 0)
        def _():
            prepare(farthest)

        @pl.when(jnp.logical_and(t >= 0, t < n_wide))
        def _():
            away(farthest, t)

        return carry

    lax.fori_loop(0, n_wide + 1, pair, 0)

    def all_wide(send, r):
        prepare(r)

        def wide(p, carry):
            send(r, p)
            return carry

        lax.fori_loop(0, n_wide, wide, 0)

    in_order(lambda r: all_wide(away, r), lambda r: all_wide(back, r), skip=True)

    prepare(z)
    for p in range(n_wide):
        own[:, p * WIDE:(p + 1) * WIDE] = corr(p)
    keep = pl.ds(pl.multiple_of(tm * rows, rows), rows)
    give = pl.ds(pl.multiple_of(other * rows, rows), rows)
    trade = pltpu.make_async_remote_copy(
        src_ref=own.at[give, :], dst_ref=ownrecv, send_sem=osem.at[0], recv_sem=osem.at[1],
        device_id=dev(z, other, blk), device_id_type=mesh_id)
    trade.start()
    out_ref[:, mine] = own[keep, :] / n_run
    trade.wait_recv()
    out_ref[:, theirs] = ownrecv[...] / n_run
    for way, present in ((0, z > 0), (1, z < n_run - 1)):

        @pl.when(present)
        def _():
            for p in range(n_wide):
                for c in range(2):
                    pltpu.make_async_copy(final.at[way, c, p], final.at[way, c, p], frecv.at[way, c, p]).wait()
                    cols = slice(c * half + p * WIDE, c * half + (p + 1) * WIDE)
                    out_ref[:, cols] += decode(final.at[way, c, p], rows) / n_run

    sswap.wait_send()
    swap.wait_send()
    trade.wait_send()

    def drain(r, carry):
        for d in range(1, n_blk):
            seed_copy(d, r).wait_send()

        next_door = jnp.logical_or(r == z - 1, r == z + 1)

        @pl.when(next_door)
        def _():
            for p in range(n_wide):
                for h in range(2):
                    deliver(r, p, h).wait_send()

        @pl.when(jnp.logical_and(r != z, jnp.logical_not(next_door)))
        def _():
            for p in range(n_wide):
                pass_on(r, p).wait_send()

        return carry

    lax.fori_loop(0, n_run, drain, 0)


def local(n_run, n_blk, series, weights, taps, lags):
    signal = series[0]
    frames, panel = signal.shape
    half = panel // 2
    fp = -(-2 * frames // 256) * 256
    n_filter = -(-(fp + LAGS) // OUT_BLK)
    rows_run = SEED_DEV // n_run * n_blk
    rows = rows_run // 2
    long, short = 2 * rows_run + 16, 2 * rows + 16
    n_wide = half // WIDE
    vmem = pl.BlockSpec(memory_space=pltpu.VMEM)
    dma = pltpu.SemaphoreType.DMA
    f32, b16 = jnp.float32, jnp.bfloat16
    flops = 2 * half * fp * (IN_BLK + n_blk * SEED_DEV)
    return pl.pallas_call(
        functools.partial(kernel, (n_run, n_blk, frames, panel, fp, n_filter)),
        out_shape=jax.ShapeDtypeStruct((rows, panel), f32),
        in_specs=[pl.BlockSpec(memory_space=pl.ANY), vmem, pl.BlockSpec(memory_space=pltpu.SMEM), vmem],
        out_specs=vmem,
        scratch_shapes=[
            pltpu.VMEM((frames, panel), b16),
            pltpu.VMEM((frames, SEED_DEV), b16),
            pltpu.VMEM((frames, SEED_DEV), b16),
            pltpu.VMEM((n_filter * OUT_BLK + IN_BLK - OUT_BLK, SEED_DEV), f32),
            pltpu.VMEM((fp, SEED_DEV), b16),
            pltpu.VMEM((frames, half), b16),
            pltpu.VMEM((n_filter * OUT_BLK + IN_BLK - OUT_BLK, half), f32),
            pltpu.VMEM((OUT_BLK, IN_BLK), b16),
            pltpu.VMEM((fp, 128), f32),
            pltpu.VMEM((fp, 128), f32),
            pltpu.VMEM((half // 128, 128), jnp.int32),
            pltpu.VMEM((n_filter * OUT_BLK, 256), f32),
            pltpu.VMEM((fp, 256), f32),
            pltpu.VMEM((fp, half), b16),
            pltpu.VMEM((n_blk, n_run, SEED_DEV // n_run, fp), b16),
            pltpu.VMEM((rows_run, fp), b16),
            pltpu.VMEM((n_run, n_wide, 2 * short, 128), jnp.int16),
            pltpu.VMEM((n_run, n_wide, long, 128), jnp.int16),
            pltpu.VMEM((2, 2, n_wide, short, 128), jnp.int16),
            pltpu.VMEM((rows_run, WIDE), f32),
            pltpu.VMEM((rows_run, half), f32),
            pltpu.VMEM((rows, half), f32),
            dma((5,)),
            dma((n_blk, n_run)),
            dma((n_blk, n_run)),
            dma((n_run, n_wide, 2)),
            dma((n_run, n_wide)),
            dma((2, 2, n_wide)),
            dma((2,)),
        ],
        compiler_params=pltpu.CompilerParams(
            collective_id=0, has_side_effects=True, vmem_limit_bytes=56 * 1024 * 1024),
        cost_estimate=pl.CostEstimate(flops=flops, bytes_accessed=2 * frames * panel, transcendentals=0),
    )(signal, weights, taps, lags.reshape(panel // 128, 128))


def solution(mesh):
    placed = (P("run", "tm", "blk"), P("run", None), P(), P("blk"))
    body = functools.partial(local, mesh.shape["run"], mesh.shape["blk"])
    return jax.shard_map(
        body, mesh=mesh, in_specs=placed, out_specs=P(("run", "tm"), "blk"), check_vma=False
    )
```

```python
import functools

import jax
import jax.numpy as jnp
from jax import lax
from jax.experimental import pallas as pl
from jax.experimental.pallas import tpu as pltpu
from jax.sharding import PartitionSpec as P

HALF = 16
LAGS = 4
SEED_DEV = 128
TAPS = 2 * HALF + 1
OUT_BLK = 224
IN_BLK = 256
CHUNK = 128
WIDE = 256
TOP = 32000.0
STEPS = 128.0
epsilon = 1e-05


def kernel(dims, x_hbm, w_ref, taps_ref, lags_ref, out_ref, x_ref, sown, sother, sfull, sscore, xrecv, xfull, toep, wcol,
           rcol, lagscr, banded, filt, scores, seeds, left, stage, transit, final, part, own, ownrecv, xsem, dsend, fsend, srecv, tsend,
           trecv, frecv, osem):
    n_run, n_blk, frames, panel, fp, n_filter = dims
    half = panel // 2
    groups = half // 128
    total_frames = 2 * frames
    q_run = SEED_DEV // n_run
    rows_run = q_run * n_blk
    rows = rows_run // 2
    runs_core = n_run // 2

    z = lax.axis_index("run")
    tm = lax.axis_index("tm")
    blk = lax.axis_index("blk")
    other = 1 - tm

    def dev(run, core, block):
        return (run, core, block)

    barrier = pltpu.get_barrier_semaphore()
    mesh_id = pl.DeviceIdType.MESH
    pl.semaphore_signal(barrier, inc=1, device_id=dev(z, other, blk), device_id_type=mesh_id)
    for d in range(1, n_blk):
        peer = lax.rem(blk + d, n_blk)
        pl.semaphore_signal(barrier, inc=1, device_id=dev(z, tm, peer), device_id_type=mesh_id)

    @pl.when(z > 0)
    def _():
        for core in range(2):
            pl.semaphore_signal(barrier, inc=1, device_id=dev(z - 1, core, blk), device_id_type=mesh_id)

    @pl.when(z < n_run - 1)
    def _():
        for core in range(2):
            pl.semaphore_signal(barrier, inc=1, device_id=dev(z + 1, core, blk), device_id_type=mesh_id)

    mine = pl.ds(pl.multiple_of(tm * half, 128), half)
    theirs = pl.ds(pl.multiple_of(other * half, 128), half)
    load = pltpu.make_async_copy(x_hbm, x_ref, xsem.at[4])
    load.start()

    diff = (lax.broadcasted_iota(jnp.int32, (OUT_BLK, IN_BLK), 1)
            - lax.broadcasted_iota(jnp.int32, (OUT_BLK, IN_BLK), 0))
    band = jnp.zeros((OUT_BLK, IN_BLK), jnp.float32)
    for k in range(TAPS):
        band = jnp.where(diff == k, taps_ref[k].astype(jnp.float32), band)
    toep[...] = band.astype(jnp.bfloat16)

    wrow = w_ref[...].astype(jnp.float32)
    total = jnp.sum(wrow)
    wrow = jnp.concatenate([wrow, jnp.zeros((1, fp - total_frames), jnp.float32)], axis=1)
    for j in range(fp // 128):
        square = jnp.broadcast_to(wrow[:, j * 128:(j + 1) * 128], (128, 128)).T
        wcol[j * 128:(j + 1) * 128, :] = square
        rcol[j * 128:(j + 1) * 128, :] = jnp.sqrt(square)

    def one_hot(mask):
        return mask.astype(jnp.float32).astype(jnp.bfloat16)

    pick = one_hot(lax.broadcasted_iota(jnp.int32, (panel, SEED_DEV), 0)
                   == (panel // SEED_DEV) * lax.broadcasted_iota(jnp.int32, (panel, SEED_DEV), 1))
    load.wait()
    sown[...] = jnp.dot(x_ref[...], pick, preferred_element_type=jnp.float32).astype(jnp.bfloat16)

    inner = jnp.logical_and(z > 0, z < n_run - 1)
    pl.semaphore_wait(barrier, jnp.where(inner, n_blk + 4, n_blk + 2))

    sswap = pltpu.make_async_remote_copy(
        src_ref=sown, dst_ref=sother, send_sem=xsem.at[2], recv_sem=xsem.at[3],
        device_id=dev(z, other, blk), device_id_type=mesh_id)
    sswap.start()
    swap = pltpu.make_async_remote_copy(
        src_ref=x_ref.at[:, theirs], dst_ref=xrecv, send_sem=xsem.at[0], recv_sem=xsem.at[1],
        device_id=dev(z, other, blk), device_id_type=mesh_id)
    swap.start()

    tail = HALF + total_frames
    near = pl.ds(pl.multiple_of(HALF + tm * frames, 8), frames)
    far_rows = pl.ds(pl.multiple_of(HALF + other * frames, 8), frames)

    def edges(ref, width):
        ref[0:HALF, :] = jnp.zeros((HALF, width), jnp.float32)
        ref[tail:, :] = jnp.zeros((ref.shape[0] - tail, width), jnp.float32)

    def normalize(src, lanes, lag, dst):
        width = lag.shape[1]
        for b in range(n_filter):
            banded[b * OUT_BLK:(b + 1) * OUT_BLK, 0:width] = jnp.dot(
                toep[...], src[b * OUT_BLK:b * OUT_BLK + IN_BLK, lanes].astype(jnp.bfloat16),
                preferred_element_type=jnp.float32)
        for g in range(width // 128):
            part = slice(g * 128, (g + 1) * 128)
            odd = jnp.broadcast_to((lag[:, part] & 1) == 1, (CHUNK + 8, 128))
            high = jnp.broadcast_to(lag[:, part] >= 2, (CHUNK, 128))
            sums = []
            for r0 in range(0, fp, CHUNK):
                late = banded[r0:r0 + CHUNK + 16, part]
                v = jnp.where(odd, late[1:CHUNK + 9], late[0:CHUNK + 8])
                v = jnp.where(high, v[2:CHUNK + 2], v[0:CHUNK])
                v = v.astype(jnp.bfloat16).astype(jnp.float32)
                filt[r0:r0 + CHUNK, part] = v
                wv = wcol[r0:r0 + CHUNK, :] * v
                sums.append((jnp.sum(wv.reshape(CHUNK // 8, 8, 128), axis=0),
                             jnp.sum((wv * v).reshape(CHUNK // 8, 8, 128), axis=0)))
            first = jnp.sum(sum(a for a, _ in sums), axis=0, keepdims=True) / total
            second = jnp.sum(sum(a for _, a in sums), axis=0, keepdims=True) / total
            scaling = lax.rsqrt(second - first * first + epsilon)
            for r0 in range(0, fp, CHUNK):
                v = rcol[r0:r0 + CHUNK, :] * (filt[r0:r0 + CHUNK, part] - first) * scaling
                dst(r0, g, v.astype(jnp.bfloat16))

    edges(sfull, SEED_DEV)
    sfull[near, :] = sown[...].astype(jnp.float32)
    lag_rows = [lags_ref[j:j + 1, :] for j in range(panel // 128)]
    lag_all = jnp.broadcast_to(jnp.concatenate(lag_rows, axis=1), (8, panel)).astype(jnp.float32)
    seed_lag = jnp.dot(lag_all.astype(jnp.bfloat16), pick, preferred_element_type=jnp.float32)
    seed_lag = seed_lag.astype(jnp.int32)[0:1, :]
    edges(xfull, half)
    xfull[near, :] = x_ref[:, mine].astype(jnp.float32)
    sswap.wait_recv()
    sfull[far_rows, :] = sother[...].astype(jnp.float32)

    def seed_store(r0, g, v):
        sscore[r0:r0 + CHUNK, :] = v

    normalize(sfull, slice(0, SEED_DEV), seed_lag, seed_store)
    eye = one_hot(lax.broadcasted_iota(jnp.int32, (SEED_DEV, SEED_DEV), 1)
                  == lax.broadcasted_iota(jnp.int32, (SEED_DEV, SEED_DEV), 0))
    rows_seed = lax.dot_general(
        eye, sscore[...], (((1,), (1,)), ((), ())), preferred_element_type=jnp.float32).astype(jnp.bfloat16)
    for r in range(n_run):
        seeds[blk, r] = rows_seed[r * q_run:(r + 1) * q_run, :]

    flip = (z >= runs_core).astype(jnp.int32)
    zz = z + flip * (n_run - 1 - 2 * z)

    def unflip(rr):
        return rr + flip * (n_run - 1 - 2 * rr)

    def turn(j):
        pairs = jnp.where(lax.rem(j, 2) == 0, n_run - 1 - lax.div(j, 2), lax.div(j, 2))
        return unflip(jnp.where(j < 2 * zz, pairs, n_run - 1 - j + zz))

    farthest = unflip(n_run - 1)

    def seed_copy(d, r):
        return pltpu.make_async_remote_copy(
            src_ref=seeds.at[blk, r], dst_ref=seeds.at[blk, r], send_sem=dsend.at[d, r],
            recv_sem=srecv.at[blk, r], device_id=dev(z, tm, lax.rem(blk + d, n_blk)), device_id_type=mesh_id)

    def relay_copy(d, r):
        peer = lax.rem(blk + n_blk - d, n_blk)
        return pltpu.make_async_remote_copy(
            src_ref=seeds.at[peer, r], dst_ref=seeds.at[peer, r], send_sem=fsend.at[d, r],
            recv_sem=srecv.at[peer, r], device_id=dev(z, other, blk), device_id_type=mesh_id)

    def arrived(d, r):
        peer = lax.rem(blk + n_blk - d, n_blk)
        pltpu.make_async_copy(seeds.at[peer, r], seeds.at[peer, r], srecv.at[peer, r]).wait()

    def carried(r):
        return jnp.logical_and(r != farthest, lax.rem(r, 2) == tm)

    def relay(r):
        @pl.when(carried(r))
        def _():
            for d in range(1, n_blk):
                arrived(d, r)
                relay_copy(d, r).start()

    for d in range(1, n_blk):
        seed_copy(d, farthest).start()

    swap.wait_recv()
    xfull[far_rows, :] = xrecv[...].astype(jnp.float32)
    lag_own = jnp.where(tm == 0, jnp.concatenate(lag_rows[:groups], axis=1),
                        jnp.concatenate(lag_rows[groups:], axis=1))
    for g in range(groups):
        lagscr[g:g + 1, :] = lag_own[:, g * 128:(g + 1) * 128]

    i = lax.broadcasted_iota(jnp.int32, (rows_run, rows_run), 0)
    j = lax.broadcasted_iota(jnp.int32, (rows_run, rows_run), 1)
    n_vec = jnp.full((rows_run, rows_run), n_blk, jnp.int32)
    order = one_hot(j == lax.rem(i, n_vec) * q_run + lax.div(i, n_vec))

    def prepare(r):
        @pl.when(jnp.logical_not(carried(r)))
        def _():
            for d in range(1, n_blk):
                arrived(d, r)

        rows_left = jnp.concatenate([seeds[b, r] for b in range(n_blk)], axis=0)
        left[...] = jnp.dot(order, rows_left, preferred_element_type=jnp.float32).astype(jnp.bfloat16)

    def corr(p):
        cols = pl.ds(pl.multiple_of(p * WIDE, WIDE), WIDE)
        return jnp.dot(left[...], scores[:, cols], preferred_element_type=jnp.float32) / total

    def encode(buf, at, v):
        count = v.shape[0]
        peak = jnp.max(jnp.abs(v), axis=0, keepdims=True)
        lane = jnp.maximum(peak[:, 0:128], peak[:, 128:256])
        code = jnp.ceil(jnp.log2(jnp.maximum(lane, 1e-30)) * STEPS) + 1.0
        gain = TOP * jnp.exp2(code * (-1.0 / STEPS))
        for g in range(2):
            scaled = jnp.round(v[:, g * 128:(g + 1) * 128] * gain)
            buf[at + g * count:at + (g + 1) * count, :] = scaled.astype(jnp.int32).astype(jnp.int16)
        at += 2 * count
        buf[at:at + 16, :] = jnp.broadcast_to(code, (16, 128)).astype(jnp.int32).astype(jnp.int16)

    def decode(buf, count):
        code = buf[2 * count:2 * count + 16, :].astype(jnp.int32).astype(jnp.float32)[0:1, :]
        unit = jnp.exp2(code * (1.0 / STEPS)) * (1.0 / TOP)
        return jnp.concatenate(
            [buf[g * count:(g + 1) * count, :].astype(jnp.int32).astype(jnp.float32) * unit for g in range(2)],
            axis=1)

    long, short = 2 * rows_run + 16, 2 * rows + 16

    def pass_on(r, p):
        nxt = jnp.where(r > z, z + 1, z - 1)
        return pltpu.make_async_remote_copy(
            src_ref=stage.at[r, p, pl.ds(0, long)], dst_ref=transit.at[r, p], send_sem=tsend.at[r, p, 0],
            recv_sem=trecv.at[r, p], device_id=dev(nxt, tm, blk), device_id_type=mesh_id)

    def deliver(r, p, h):
        way = jnp.where(r > z, 0, 1)
        return pltpu.make_async_remote_copy(
            src_ref=stage.at[r, p, pl.ds(h * short, short)], dst_ref=final.at[way, tm, p],
            send_sem=tsend.at[r, p, h], recv_sem=frecv.at[way, tm, p],
            device_id=dev(r, h, blk), device_id_type=mesh_id)

    def send_block(r, p):
        up = r > z
        nxt = jnp.where(up, z + 1, z - 1)
        part[...] = corr(p)

        @pl.when(jnp.logical_or(jnp.logical_and(up, z > 0), jnp.logical_and(r < z, z < n_run - 1)))
        def _():
            pltpu.make_async_copy(transit.at[r, p], transit.at[r, p], trecv.at[r, p]).wait()
            part[...] += decode(transit.at[r, p], rows_run)

        def after():
            @pl.when(jnp.logical_and(r != 0, r != n_run - 1))
            def _():
                pass_on(jnp.where(up, r + 1, r - 1), p).wait_send()

        @pl.when(r == nxt)
        def _():
            for h in range(2):
                encode(stage.at[r, p], h * short, part[h * rows:(h + 1) * rows, :])
            after()
            for h in range(2):
                deliver(r, p, h).start()

        @pl.when(r != nxt)
        def _():
            encode(stage.at[r, p], 0, part[...])
            after()
            pass_on(r, p).start()

    n_wide = half // WIDE
    late = (zz > 0).astype(jnp.int32)

    def pair(p, carry):
        @pl.when(p < n_wide)
        def _():
            lane0 = pl.multiple_of(p * WIDE, WIDE)
            lag = jnp.concatenate([lagscr[pl.ds(2 * p, 1), :], lagscr[pl.ds(2 * p + 1, 1), :]], axis=1)

            def store(r0, g, v):
                scores[r0:r0 + CHUNK, pl.ds(pl.multiple_of(lane0 + g * 128, 128), 128)] = v

            normalize(xfull, pl.ds(lane0, WIDE), lag, store)

        @pl.when(p == 0)
        def _():
            def send_rest(j, carry):
                r = turn(j)

                @pl.when(carried(r))
                def _():
                    for d in range(1, n_blk):
                        seed_copy(d, r).start()

                return carry

            lax.fori_loop(1, n_run, send_rest, 0)

        t = p - late

        @pl.when(t == 0)
        def _():
            prepare(farthest)

        @pl.when(jnp.logical_and(t >= 0, t < n_wide))
        def _():
            send_block(farthest, t)

        return carry

    lax.fori_loop(0, n_wide + 1, pair, 0)

    relay(turn(1))

    def send_run(j, carry):
        r = turn(j)
        prepare(r)

        def wide(p, carry):
            @pl.when(p == n_wide - 1)
            def _():
                relay(turn(j + 1))

            send_block(r, p)
            return carry

        lax.fori_loop(0, n_wide, wide, 0)
        return carry

    lax.fori_loop(1, n_run - 1, send_run, 0)

    prepare(z)
    for p in range(n_wide):
        own[:, p * WIDE:(p + 1) * WIDE] = corr(p)
    keep = pl.ds(pl.multiple_of(tm * rows, rows), rows)
    give = pl.ds(pl.multiple_of(other * rows, rows), rows)
    trade = pltpu.make_async_remote_copy(
        src_ref=own.at[give, :], dst_ref=ownrecv, send_sem=osem.at[0], recv_sem=osem.at[1],
        device_id=dev(z, other, blk), device_id_type=mesh_id)
    trade.start()
    out_ref[:, mine] = own[keep, :] / n_run
    trade.wait_recv()
    out_ref[:, theirs] = ownrecv[...] / n_run
    for way, present in ((0, z > 0), (1, z < n_run - 1)):

        @pl.when(present)
        def _():
            for p in range(n_wide):
                for c in range(2):
                    pltpu.make_async_copy(final.at[way, c, p], final.at[way, c, p], frecv.at[way, c, p]).wait()
                    cols = slice(c * half + p * WIDE, c * half + (p + 1) * WIDE)
                    out_ref[:, cols] += decode(final.at[way, c, p], rows) / n_run

    sswap.wait_send()
    swap.wait_send()
    trade.wait_send()

    def drain(r, carry):
        @pl.when(jnp.logical_or(carried(r), r == farthest))
        def _():
            for d in range(1, n_blk):
                seed_copy(d, r).wait_send()

        @pl.when(carried(r))
        def _():
            for d in range(1, n_blk):
                relay_copy(d, r).wait_send()

        @pl.when(jnp.logical_or(r == z - 1, r == z + 1))
        def _():
            for p in range(n_wide):
                for h in range(2):
                    deliver(r, p, h).wait_send()

        return carry

    lax.fori_loop(0, n_run, drain, 0)


def local(n_run, n_blk, series, weights, taps, lags):
    signal = series[0]
    frames, panel = signal.shape
    half = panel // 2
    fp = -(-2 * frames // 256) * 256
    n_filter = -(-(fp + LAGS) // OUT_BLK)
    rows_run = SEED_DEV // n_run * n_blk
    rows = rows_run // 2
    long, short = 2 * rows_run + 16, 2 * rows + 16
    n_wide = half // WIDE
    vmem = pl.BlockSpec(memory_space=pltpu.VMEM)
    dma = pltpu.SemaphoreType.DMA
    f32, b16 = jnp.float32, jnp.bfloat16
    flops = 2 * half * fp * (IN_BLK + n_blk * SEED_DEV)
    return pl.pallas_call(
        functools.partial(kernel, (n_run, n_blk, frames, panel, fp, n_filter)),
        out_shape=jax.ShapeDtypeStruct((rows, panel), f32),
        in_specs=[pl.BlockSpec(memory_space=pl.ANY), vmem, pl.BlockSpec(memory_space=pltpu.SMEM), vmem],
        out_specs=vmem,
        scratch_shapes=[
            pltpu.VMEM((frames, panel), b16),
            pltpu.VMEM((frames, SEED_DEV), b16),
            pltpu.VMEM((frames, SEED_DEV), b16),
            pltpu.VMEM((n_filter * OUT_BLK + IN_BLK - OUT_BLK, SEED_DEV), f32),
            pltpu.VMEM((fp, SEED_DEV), b16),
            pltpu.VMEM((frames, half), b16),
            pltpu.VMEM((n_filter * OUT_BLK + IN_BLK - OUT_BLK, half), f32),
            pltpu.VMEM((OUT_BLK, IN_BLK), b16),
            pltpu.VMEM((fp, 128), f32),
            pltpu.VMEM((fp, 128), f32),
            pltpu.VMEM((half // 128, 128), jnp.int32),
            pltpu.VMEM((n_filter * OUT_BLK, 256), f32),
            pltpu.VMEM((fp, 256), f32),
            pltpu.VMEM((fp, half), b16),
            pltpu.VMEM((n_blk, n_run, SEED_DEV // n_run, fp), b16),
            pltpu.VMEM((rows_run, fp), b16),
            pltpu.VMEM((n_run, n_wide, 2 * short, 128), jnp.int16),
            pltpu.VMEM((n_run, n_wide, long, 128), jnp.int16),
            pltpu.VMEM((2, 2, n_wide, short, 128), jnp.int16),
            pltpu.VMEM((rows_run, WIDE), f32),
            pltpu.VMEM((rows_run, half), f32),
            pltpu.VMEM((rows, half), f32),
            dma((5,)),
            dma((n_blk, n_run)),
            dma((n_blk, n_run)),
            dma((n_blk, n_run)),
            dma((n_run, n_wide, 2)),
            dma((n_run, n_wide)),
            dma((2, 2, n_wide)),
            dma((2,)),
        ],
        compiler_params=pltpu.CompilerParams(
            collective_id=0, has_side_effects=True, vmem_limit_bytes=56 * 1024 * 1024),
        cost_estimate=pl.CostEstimate(flops=flops, bytes_accessed=2 * frames * panel, transcendentals=0),
    )(signal, weights, taps, lags.reshape(panel // 128, 128))


def solution(mesh):
    placed = (P("run", "tm", "blk"), P("run", None), P(), P("blk"))
    body = functools.partial(local, mesh.shape["run"], mesh.shape["blk"])
    return jax.shard_map(
        body, mesh=mesh, in_specs=placed, out_specs=P(("run", "tm"), "blk"), check_vma=False
    )
```

```python
import functools

import jax
import jax.numpy as jnp
from jax import lax
from jax.experimental import pallas as pl
from jax.experimental.pallas import tpu as pltpu
from jax.sharding import PartitionSpec as P

HALF = 16
LAGS = 4
SEED_DEV = 128
TAPS = 2 * HALF + 1
OUT_BLK = 224
IN_BLK = 256
CHUNK = 128
WIDE = 256
TOP = 32000.0
STEPS = 128.0
epsilon = 1e-05


def kernel(dims, x_hbm, w_ref, taps_ref, lags_ref, out_ref, x_ref, sown, sother, sfull, sscore, xrecv, xfull, toep, wcol,
           rcol, lagscr, banded, filt, scores, seeds, left, stage, transit, final, part, own, ownrecv, xsem, dsend, srecv, tsend,
           trecv, frecv, osem):
    n_run, n_blk, frames, panel, fp, n_filter = dims
    half = panel // 2
    groups = half // 128
    total_frames = 2 * frames
    q_run = SEED_DEV // n_run
    rows_run = q_run * n_blk
    rows = rows_run // 2
    runs_core = n_run // 2

    z = lax.axis_index("run")
    tm = lax.axis_index("tm")
    blk = lax.axis_index("blk")
    other = 1 - tm

    def dev(run, core, block):
        return (run, core, block)

    barrier = pltpu.get_barrier_semaphore()
    mesh_id = pl.DeviceIdType.MESH
    pl.semaphore_signal(barrier, inc=1, device_id=dev(z, other, blk), device_id_type=mesh_id)
    for d in range(1, n_blk):
        peer = lax.rem(blk + d, n_blk)
        pl.semaphore_signal(barrier, inc=1, device_id=dev(z, tm, peer), device_id_type=mesh_id)

    @pl.when(z > 0)
    def _():
        for core in range(2):
            pl.semaphore_signal(barrier, inc=1, device_id=dev(z - 1, core, blk), device_id_type=mesh_id)

    @pl.when(z < n_run - 1)
    def _():
        for core in range(2):
            pl.semaphore_signal(barrier, inc=1, device_id=dev(z + 1, core, blk), device_id_type=mesh_id)

    mine = pl.ds(pl.multiple_of(tm * half, 128), half)
    theirs = pl.ds(pl.multiple_of(other * half, 128), half)
    load = pltpu.make_async_copy(x_hbm, x_ref, xsem.at[4])
    load.start()

    def one_hot(mask):
        return mask.astype(jnp.float32).astype(jnp.bfloat16)

    pick = one_hot(lax.broadcasted_iota(jnp.int32, (panel, SEED_DEV), 0)
                   == (panel // SEED_DEV) * lax.broadcasted_iota(jnp.int32, (panel, SEED_DEV), 1))
    load.wait()
    sown[...] = jnp.dot(x_ref[...], pick, preferred_element_type=jnp.float32).astype(jnp.bfloat16)

    inner = jnp.logical_and(z > 0, z < n_run - 1)
    pl.semaphore_wait(barrier, jnp.where(inner, n_blk + 4, n_blk + 2))

    sswap = pltpu.make_async_remote_copy(
        src_ref=sown, dst_ref=sother, send_sem=xsem.at[2], recv_sem=xsem.at[3],
        device_id=dev(z, other, blk), device_id_type=mesh_id)
    sswap.start()
    swap = pltpu.make_async_remote_copy(
        src_ref=x_ref.at[:, theirs], dst_ref=xrecv, send_sem=xsem.at[0], recv_sem=xsem.at[1],
        device_id=dev(z, other, blk), device_id_type=mesh_id)
    swap.start()

    lane = lax.broadcasted_iota(jnp.int32, (8, IN_BLK), 1)
    row = jnp.zeros((8, IN_BLK), jnp.float32)
    for k in range(TAPS):
        row = jnp.where(lane == k, taps_ref[k].astype(jnp.float32), row)
    band = jnp.broadcast_to(row[0:1, :], (OUT_BLK, IN_BLK))
    toep[...] = pltpu.roll(band, 0, 1, stride=1, stride_axis=0).astype(jnp.bfloat16)

    wrow = w_ref[...].astype(jnp.float32)
    total = jnp.sum(wrow)
    wrow = jnp.concatenate([wrow, jnp.zeros((1, fp - total_frames), jnp.float32)], axis=1)
    for j in range(fp // 128):
        square = jnp.broadcast_to(wrow[:, j * 128:(j + 1) * 128], (128, 128)).T
        wcol[j * 128:(j + 1) * 128, :] = square
        rcol[j * 128:(j + 1) * 128, :] = jnp.sqrt(square)

    tail = HALF + total_frames
    near = pl.ds(pl.multiple_of(HALF + tm * frames, 8), frames)
    far_rows = pl.ds(pl.multiple_of(HALF + other * frames, 8), frames)

    def edges(ref, width):
        ref[0:HALF, :] = jnp.zeros((HALF, width), jnp.float32)
        ref[tail:, :] = jnp.zeros((ref.shape[0] - tail, width), jnp.float32)

    def normalize(src, lanes, lag, dst):
        width = lag.shape[1]
        for b in range(n_filter):
            banded[b * OUT_BLK:(b + 1) * OUT_BLK, 0:width] = jnp.dot(
                toep[...], src[b * OUT_BLK:b * OUT_BLK + IN_BLK, lanes].astype(jnp.bfloat16),
                preferred_element_type=jnp.float32)
        for g in range(width // 128):
            part = slice(g * 128, (g + 1) * 128)
            odd = jnp.broadcast_to((lag[:, part] & 1) == 1, (CHUNK + 8, 128))
            high = jnp.broadcast_to(lag[:, part] >= 2, (CHUNK, 128))
            sums = []
            for r0 in range(0, fp, CHUNK):
                late = banded[r0:r0 + CHUNK + 16, part]
                v = jnp.where(odd, late[1:CHUNK + 9], late[0:CHUNK + 8])
                v = jnp.where(high, v[2:CHUNK + 2], v[0:CHUNK])
                v = v.astype(jnp.bfloat16).astype(jnp.float32)
                filt[r0:r0 + CHUNK, part] = v
                wv = wcol[r0:r0 + CHUNK, :] * v
                sums.append((jnp.sum(wv.reshape(CHUNK // 8, 8, 128), axis=0),
                             jnp.sum((wv * v).reshape(CHUNK // 8, 8, 128), axis=0)))
            first = jnp.sum(sum(a for a, _ in sums), axis=0, keepdims=True) / total
            second = jnp.sum(sum(a for _, a in sums), axis=0, keepdims=True) / total
            scaling = lax.rsqrt(second - first * first + epsilon)
            for r0 in range(0, fp, CHUNK):
                v = rcol[r0:r0 + CHUNK, :] * (filt[r0:r0 + CHUNK, part] - first) * scaling
                dst(r0, g, v.astype(jnp.bfloat16))

    edges(sfull, SEED_DEV)
    sfull[near, :] = sown[...].astype(jnp.float32)
    lag_rows = [lags_ref[j:j + 1, :] for j in range(panel // 128)]
    lag_all = jnp.broadcast_to(jnp.concatenate(lag_rows, axis=1), (8, panel)).astype(jnp.float32)
    seed_lag = jnp.dot(lag_all.astype(jnp.bfloat16), pick, preferred_element_type=jnp.float32)
    seed_lag = seed_lag.astype(jnp.int32)[0:1, :]
    edges(xfull, half)
    xfull[near, :] = x_ref[:, mine].astype(jnp.float32)
    sswap.wait_recv()
    sfull[far_rows, :] = sother[...].astype(jnp.float32)

    def seed_store(r0, g, v):
        sscore[r0:r0 + CHUNK, :] = v

    normalize(sfull, slice(0, SEED_DEV), seed_lag, seed_store)
    eye = one_hot(lax.broadcasted_iota(jnp.int32, (SEED_DEV, SEED_DEV), 1)
                  == lax.broadcasted_iota(jnp.int32, (SEED_DEV, SEED_DEV), 0))
    rows_seed = lax.dot_general(
        eye, sscore[...], (((1,), (1,)), ((), ())), preferred_element_type=jnp.float32).astype(jnp.bfloat16)
    for r in range(n_run):
        seeds[blk, r] = rows_seed[r * q_run:(r + 1) * q_run, :]

    flip = (z >= runs_core).astype(jnp.int32)
    zz = z + flip * (n_run - 1 - 2 * z)

    def unflip(rr):
        return rr + flip * (n_run - 1 - 2 * rr)

    def turn(j):
        pairs = jnp.where(lax.rem(j, 2) == 0, n_run - 1 - lax.div(j, 2), lax.div(j, 2))
        return unflip(jnp.where(j < 2 * zz, pairs, n_run - 1 - j + zz))

    farthest = unflip(n_run - 1)

    def seed_copy(d, r):
        return pltpu.make_async_remote_copy(
            src_ref=seeds.at[blk, r], dst_ref=seeds.at[blk, r], send_sem=dsend.at[d, r],
            recv_sem=srecv.at[blk, r], device_id=dev(z, tm, lax.rem(blk + d, n_blk)), device_id_type=mesh_id)

    def arrived(d, r):
        peer = lax.rem(blk + n_blk - d, n_blk)
        pltpu.make_async_copy(seeds.at[peer, r], seeds.at[peer, r], srecv.at[peer, r]).wait()

    def send_seeds(r):
        for d in range(1, n_blk):
            seed_copy(d, r).start()

    send_seeds(farthest)

    swap.wait_recv()
    xfull[far_rows, :] = xrecv[...].astype(jnp.float32)
    lag_own = jnp.where(tm == 0, jnp.concatenate(lag_rows[:groups], axis=1),
                        jnp.concatenate(lag_rows[groups:], axis=1))
    for g in range(groups):
        lagscr[g:g + 1, :] = lag_own[:, g * 128:(g + 1) * 128]

    i = lax.broadcasted_iota(jnp.int32, (rows_run, rows_run), 0)
    j = lax.broadcasted_iota(jnp.int32, (rows_run, rows_run), 1)
    n_vec = jnp.full((rows_run, rows_run), n_blk, jnp.int32)
    order = one_hot(j == lax.rem(i, n_vec) * q_run + lax.div(i, n_vec))

    def prepare(r):
        for d in range(1, n_blk):
            arrived(d, r)
        rows_left = jnp.concatenate([seeds[b, r] for b in range(n_blk)], axis=0)
        left[...] = jnp.dot(order, rows_left, preferred_element_type=jnp.float32).astype(jnp.bfloat16)

    def corr(p):
        cols = pl.ds(pl.multiple_of(p * WIDE, WIDE), WIDE)
        return jnp.dot(left[...], scores[:, cols], preferred_element_type=jnp.float32) / total

    def encode(buf, at, v):
        count = v.shape[0]
        peak = jnp.max(jnp.abs(v), axis=0, keepdims=True)
        lane = jnp.maximum(peak[:, 0:128], peak[:, 128:256])
        code = jnp.ceil(jnp.log2(jnp.maximum(lane, 1e-30)) * STEPS) + 1.0
        gain = TOP * jnp.exp2(code * (-1.0 / STEPS))
        for g in range(2):
            scaled = jnp.round(v[:, g * 128:(g + 1) * 128] * gain)
            buf[at + g * count:at + (g + 1) * count, :] = scaled.astype(jnp.int32).astype(jnp.int16)
        at += 2 * count
        buf[at:at + 16, :] = jnp.broadcast_to(code, (16, 128)).astype(jnp.int32).astype(jnp.int16)

    def decode(buf, count):
        code = buf[2 * count:2 * count + 16, :].astype(jnp.int32).astype(jnp.float32)[0:1, :]
        unit = jnp.exp2(code * (1.0 / STEPS)) * (1.0 / TOP)
        return jnp.concatenate(
            [buf[g * count:(g + 1) * count, :].astype(jnp.int32).astype(jnp.float32) * unit for g in range(2)],
            axis=1)

    long, short = 2 * rows_run + 16, 2 * rows + 16

    def pass_on(r, p):
        nxt = jnp.where(r > z, z + 1, z - 1)
        return pltpu.make_async_remote_copy(
            src_ref=stage.at[r, p, pl.ds(0, long)], dst_ref=transit.at[r, p], send_sem=tsend.at[r, p, 0],
            recv_sem=trecv.at[r, p], device_id=dev(nxt, tm, blk), device_id_type=mesh_id)

    def deliver(r, p, h):
        way = jnp.where(r > z, 0, 1)
        return pltpu.make_async_remote_copy(
            src_ref=stage.at[r, p, pl.ds(h * short, short)], dst_ref=final.at[way, tm, p],
            send_sem=tsend.at[r, p, h], recv_sem=frecv.at[way, tm, p],
            device_id=dev(r, h, blk), device_id_type=mesh_id)

    def send_block(r, p):
        up = r > z
        nxt = jnp.where(up, z + 1, z - 1)
        part[...] = corr(p)

        @pl.when(jnp.logical_or(jnp.logical_and(up, z > 0), jnp.logical_and(r < z, z < n_run - 1)))
        def _():
            pltpu.make_async_copy(transit.at[r, p], transit.at[r, p], trecv.at[r, p]).wait()
            part[...] += decode(transit.at[r, p], rows_run)

        def after():
            @pl.when(jnp.logical_and(r != 0, r != n_run - 1))
            def _():
                pass_on(jnp.where(up, r + 1, r - 1), p).wait_send()

        @pl.when(r == nxt)
        def _():
            for h in range(2):
                encode(stage.at[r, p], h * short, part[h * rows:(h + 1) * rows, :])
            after()
            for h in range(2):
                deliver(r, p, h).start()

        @pl.when(r != nxt)
        def _():
            encode(stage.at[r, p], 0, part[...])
            after()
            pass_on(r, p).start()

    n_wide = half // WIDE
    late = (zz > 0).astype(jnp.int32)

    def pair(p, carry):
        @pl.when(p < n_wide)
        def _():
            lane0 = pl.multiple_of(p * WIDE, WIDE)
            lag = jnp.concatenate([lagscr[pl.ds(2 * p, 1), :], lagscr[pl.ds(2 * p + 1, 1), :]], axis=1)

            def store(r0, g, v):
                scores[r0:r0 + CHUNK, pl.ds(pl.multiple_of(lane0 + g * 128, 128), 128)] = v

            normalize(xfull, pl.ds(lane0, WIDE), lag, store)

        @pl.when(p == 0)
        def _():
            send_seeds(turn(1))

        t = p - late

        @pl.when(t == 0)
        def _():
            prepare(farthest)

        @pl.when(jnp.logical_and(t >= 0, t < n_wide))
        def _():
            send_block(farthest, t)

        return carry

    lax.fori_loop(0, n_wide + 1, pair, 0)

    send_seeds(turn(2))

    def send_run(j, carry):
        r = turn(j)

        @pl.when(j + 2 < n_run)
        def _():
            send_seeds(turn(j + 2))

        prepare(r)

        def wide(p, carry):
            send_block(r, p)
            return carry

        lax.fori_loop(0, n_wide, wide, 0)
        return carry

    lax.fori_loop(1, n_run - 1, send_run, 0)

    prepare(z)
    for p in range(n_wide):
        own[:, p * WIDE:(p + 1) * WIDE] = corr(p)
    keep = pl.ds(pl.multiple_of(tm * rows, rows), rows)
    give = pl.ds(pl.multiple_of(other * rows, rows), rows)
    trade = pltpu.make_async_remote_copy(
        src_ref=own.at[give, :], dst_ref=ownrecv, send_sem=osem.at[0], recv_sem=osem.at[1],
        device_id=dev(z, other, blk), device_id_type=mesh_id)
    trade.start()
    out_ref[:, mine] = own[keep, :] / n_run
    trade.wait_recv()
    out_ref[:, theirs] = ownrecv[...] / n_run
    for way, present in ((0, z > 0), (1, z < n_run - 1)):

        @pl.when(present)
        def _():
            for p in range(n_wide):
                for c in range(2):
                    pltpu.make_async_copy(final.at[way, c, p], final.at[way, c, p], frecv.at[way, c, p]).wait()
                    cols = slice(c * half + p * WIDE, c * half + (p + 1) * WIDE)
                    out_ref[:, cols] += decode(final.at[way, c, p], rows) / n_run

    sswap.wait_send()
    swap.wait_send()
    trade.wait_send()

    def drain(r, carry):
        for d in range(1, n_blk):
            seed_copy(d, r).wait_send()

        @pl.when(jnp.logical_or(r == z - 1, r == z + 1))
        def _():
            for p in range(n_wide):
                for h in range(2):
                    deliver(r, p, h).wait_send()

        return carry

    lax.fori_loop(0, n_run, drain, 0)


def local(n_run, n_blk, series, weights, taps, lags):
    signal = series[0]
    frames, panel = signal.shape
    half = panel // 2
    fp = -(-2 * frames // 256) * 256
    n_filter = -(-(fp + LAGS) // OUT_BLK)
    rows_run = SEED_DEV // n_run * n_blk
    rows = rows_run // 2
    long, short = 2 * rows_run + 16, 2 * rows + 16
    n_wide = half // WIDE
    vmem = pl.BlockSpec(memory_space=pltpu.VMEM)
    dma = pltpu.SemaphoreType.DMA
    f32, b16 = jnp.float32, jnp.bfloat16
    flops = 2 * half * fp * (IN_BLK + n_blk * SEED_DEV)
    return pl.pallas_call(
        functools.partial(kernel, (n_run, n_blk, frames, panel, fp, n_filter)),
        out_shape=pltpu.VMEM((rows, panel), f32),
        in_specs=[pl.BlockSpec(memory_space=pl.ANY), vmem, pl.BlockSpec(memory_space=pltpu.SMEM), vmem],
        out_specs=vmem,
        scratch_shapes=[
            pltpu.VMEM((frames, panel), b16),
            pltpu.VMEM((frames, SEED_DEV), b16),
            pltpu.VMEM((frames, SEED_DEV), b16),
            pltpu.VMEM((n_filter * OUT_BLK + IN_BLK - OUT_BLK, SEED_DEV), f32),
            pltpu.VMEM((fp, SEED_DEV), b16),
            pltpu.VMEM((frames, half), b16),
            pltpu.VMEM((n_filter * OUT_BLK + IN_BLK - OUT_BLK, half), f32),
            pltpu.VMEM((OUT_BLK, IN_BLK), b16),
            pltpu.VMEM((fp, 128), f32),
            pltpu.VMEM((fp, 128), f32),
            pltpu.VMEM((half // 128, 128), jnp.int32),
            pltpu.VMEM((n_filter * OUT_BLK, 256), f32),
            pltpu.VMEM((fp, 256), f32),
            pltpu.VMEM((fp, half), b16),
            pltpu.VMEM((n_blk, n_run, SEED_DEV // n_run, fp), b16),
            pltpu.VMEM((rows_run, fp), b16),
            pltpu.VMEM((n_run, n_wide, 2 * short, 128), jnp.int16),
            pltpu.VMEM((n_run, n_wide, long, 128), jnp.int16),
            pltpu.VMEM((2, 2, n_wide, short, 128), jnp.int16),
            pltpu.VMEM((rows_run, WIDE), f32),
            pltpu.VMEM((rows_run, half), f32),
            pltpu.VMEM((rows, half), f32),
            dma((5,)),
            dma((n_blk, n_run)),
            dma((n_blk, n_run)),
            dma((n_run, n_wide, 2)),
            dma((n_run, n_wide)),
            dma((2, 2, n_wide)),
            dma((2,)),
        ],
        compiler_params=pltpu.CompilerParams(
            collective_id=0, has_side_effects=True, vmem_limit_bytes=56 * 1024 * 1024),
        cost_estimate=pl.CostEstimate(flops=flops, bytes_accessed=2 * frames * panel, transcendentals=0),
    )(signal, weights, taps, lags.reshape(panel // 128, 128))


def solution(mesh):
    placed = (P("run", "tm", "blk"), P("run", None), P(), P("blk"))
    body = functools.partial(local, mesh.shape["run"], mesh.shape["blk"])
    return jax.shard_map(
        body, mesh=mesh, in_specs=placed, out_specs=P(("run", "tm"), "blk"), check_vma=False
    )
```

```python
import functools

import jax
import jax.numpy as jnp
from jax import lax
from jax.experimental import pallas as pl
from jax.experimental.pallas import tpu as pltpu
from jax.sharding import PartitionSpec as P

HALF = 16
LAGS = 4
SEED_DEV = 128
TAPS = 2 * HALF + 1
OUT_BLK = 224
IN_BLK = 256
CHUNK = 128
WIDE = 256
TOP = 32000.0
STEPS = 128.0
epsilon = 1e-05


def kernel(dims, x_hbm, w_ref, taps_ref, lags_ref, out_ref, x_ref, sown, sother, sfull, sscore, xrecv, xfull, toep, wcol,
           rcol, lagscr, banded, filt, scores, seeds, left, stage, transit, final, part, own, ownrecv, xsem, dsend, srecv, tsend,
           trecv, frecv, osem):
    n_run, n_blk, frames, panel, fp, n_filter = dims
    half = panel // 2
    groups = half // 128
    total_frames = 2 * frames
    q_run = SEED_DEV // n_run
    rows_run = q_run * n_blk
    rows = rows_run // 2
    runs_core = n_run // 2

    z = lax.axis_index("run")
    tm = lax.axis_index("tm")
    blk = lax.axis_index("blk")
    other = 1 - tm

    def dev(run, core, block):
        return (run, core, block)

    barrier = pltpu.get_barrier_semaphore()
    mesh_id = pl.DeviceIdType.MESH
    pl.semaphore_signal(barrier, inc=1, device_id=dev(z, other, blk), device_id_type=mesh_id)
    for d in range(1, n_blk):
        peer = lax.rem(blk + d, n_blk)
        pl.semaphore_signal(barrier, inc=1, device_id=dev(z, tm, peer), device_id_type=mesh_id)

    @pl.when(z > 0)
    def _():
        for core in range(2):
            pl.semaphore_signal(barrier, inc=1, device_id=dev(z - 1, core, blk), device_id_type=mesh_id)

    @pl.when(z < n_run - 1)
    def _():
        for core in range(2):
            pl.semaphore_signal(barrier, inc=1, device_id=dev(z + 1, core, blk), device_id_type=mesh_id)

    mine = pl.ds(pl.multiple_of(tm * half, 128), half)
    theirs = pl.ds(pl.multiple_of(other * half, 128), half)
    load = pltpu.make_async_copy(x_hbm, x_ref, xsem.at[4])
    load.start()

    wrow = w_ref[...].astype(jnp.float32)
    total = jnp.sum(wrow)
    wrow = jnp.concatenate([wrow, jnp.zeros((1, fp - total_frames), jnp.float32)], axis=1)
    for j in range(fp // 128):
        square = jnp.broadcast_to(wrow[:, j * 128:(j + 1) * 128], (128, 128)).T
        wcol[j * 128:(j + 1) * 128, :] = square
        rcol[j * 128:(j + 1) * 128, :] = jnp.sqrt(square)

    def one_hot(mask):
        return mask.astype(jnp.float32).astype(jnp.bfloat16)

    pick = one_hot(lax.broadcasted_iota(jnp.int32, (panel, SEED_DEV), 0)
                   == (panel // SEED_DEV) * lax.broadcasted_iota(jnp.int32, (panel, SEED_DEV), 1))
    load.wait()
    sown[...] = jnp.dot(x_ref[...], pick, preferred_element_type=jnp.float32).astype(jnp.bfloat16)

    inner = jnp.logical_and(z > 0, z < n_run - 1)
    pl.semaphore_wait(barrier, jnp.where(inner, n_blk + 4, n_blk + 2))

    sswap = pltpu.make_async_remote_copy(
        src_ref=sown, dst_ref=sother, send_sem=xsem.at[2], recv_sem=xsem.at[3],
        device_id=dev(z, other, blk), device_id_type=mesh_id)
    sswap.start()
    swap = pltpu.make_async_remote_copy(
        src_ref=x_ref.at[:, theirs], dst_ref=xrecv, send_sem=xsem.at[0], recv_sem=xsem.at[1],
        device_id=dev(z, other, blk), device_id_type=mesh_id)
    swap.start()

    lane = lax.broadcasted_iota(jnp.int32, (8, IN_BLK), 1)
    row = jnp.zeros((8, IN_BLK), jnp.float32)
    for k in range(TAPS):
        row = jnp.where(lane == k, taps_ref[k].astype(jnp.float32), row)
    band = jnp.broadcast_to(row[0:1, :], (OUT_BLK, IN_BLK))
    toep[...] = pltpu.roll(band, 0, 1, stride=1, stride_axis=0).astype(jnp.bfloat16)

    tail = HALF + total_frames
    near = pl.ds(pl.multiple_of(HALF + tm * frames, 8), frames)
    far_rows = pl.ds(pl.multiple_of(HALF + other * frames, 8), frames)

    def edges(ref, width):
        ref[0:HALF, :] = jnp.zeros((HALF, width), jnp.float32)
        ref[tail:, :] = jnp.zeros((ref.shape[0] - tail, width), jnp.float32)

    def normalize(src, lanes, lag, dst):
        width = lag.shape[1]
        for b in range(n_filter):
            banded[b * OUT_BLK:(b + 1) * OUT_BLK, 0:width] = jnp.dot(
                toep[...], src[b * OUT_BLK:b * OUT_BLK + IN_BLK, lanes].astype(jnp.bfloat16),
                preferred_element_type=jnp.float32)
        for g in range(width // 128):
            part = slice(g * 128, (g + 1) * 128)
            odd = jnp.broadcast_to((lag[:, part] & 1) == 1, (CHUNK + 8, 128))
            high = jnp.broadcast_to(lag[:, part] >= 2, (CHUNK, 128))
            sums = []
            for r0 in range(0, fp, CHUNK):
                late = banded[r0:r0 + CHUNK + 16, part]
                v = jnp.where(odd, late[1:CHUNK + 9], late[0:CHUNK + 8])
                v = jnp.where(high, v[2:CHUNK + 2], v[0:CHUNK])
                v = v.astype(jnp.bfloat16).astype(jnp.float32)
                filt[r0:r0 + CHUNK, part] = v
                wv = wcol[r0:r0 + CHUNK, :] * v
                sums.append((jnp.sum(wv.reshape(CHUNK // 8, 8, 128), axis=0),
                             jnp.sum((wv * v).reshape(CHUNK // 8, 8, 128), axis=0)))
            first = jnp.sum(sum(a for a, _ in sums), axis=0, keepdims=True) / total
            second = jnp.sum(sum(a for _, a in sums), axis=0, keepdims=True) / total
            scaling = lax.rsqrt(second - first * first + epsilon)
            for r0 in range(0, fp, CHUNK):
                v = rcol[r0:r0 + CHUNK, :] * (filt[r0:r0 + CHUNK, part] - first) * scaling
                dst(r0, g, v.astype(jnp.bfloat16))

    edges(sfull, SEED_DEV)
    sfull[near, :] = sown[...].astype(jnp.float32)
    lag_rows = [lags_ref[j:j + 1, :] for j in range(panel // 128)]
    lag_all = jnp.broadcast_to(jnp.concatenate(lag_rows, axis=1), (8, panel)).astype(jnp.float32)
    seed_lag = jnp.dot(lag_all.astype(jnp.bfloat16), pick, preferred_element_type=jnp.float32)
    seed_lag = seed_lag.astype(jnp.int32)[0:1, :]
    sswap.wait_recv()
    sfull[far_rows, :] = sother[...].astype(jnp.float32)

    def seed_store(r0, g, v):
        sscore[r0:r0 + CHUNK, :] = v

    normalize(sfull, slice(0, SEED_DEV), seed_lag, seed_store)
    eye = one_hot(lax.broadcasted_iota(jnp.int32, (SEED_DEV, SEED_DEV), 1)
                  == lax.broadcasted_iota(jnp.int32, (SEED_DEV, SEED_DEV), 0))
    rows_seed = lax.dot_general(
        eye, sscore[...], (((1,), (1,)), ((), ())), preferred_element_type=jnp.float32).astype(jnp.bfloat16)
    for r in range(n_run):
        seeds[blk, r] = rows_seed[r * q_run:(r + 1) * q_run, :]

    flip = (z >= runs_core).astype(jnp.int32)
    zz = z + flip * (n_run - 1 - 2 * z)

    def unflip(rr):
        return rr + flip * (n_run - 1 - 2 * rr)

    def turn(j):
        pairs = jnp.where(lax.rem(j, 2) == 0, n_run - 1 - lax.div(j, 2), lax.div(j, 2))
        return unflip(jnp.where(j < 2 * zz, pairs, n_run - 1 - j + zz))

    farthest = unflip(n_run - 1)

    def seed_copy(d, r):
        return pltpu.make_async_remote_copy(
            src_ref=seeds.at[blk, r], dst_ref=seeds.at[blk, r], send_sem=dsend.at[d, r],
            recv_sem=srecv.at[blk, r], device_id=dev(z, tm, lax.rem(blk + d, n_blk)), device_id_type=mesh_id)

    def arrived(d, r):
        peer = lax.rem(blk + n_blk - d, n_blk)
        pltpu.make_async_copy(seeds.at[peer, r], seeds.at[peer, r], srecv.at[peer, r]).wait()

    def send_seeds(r):
        for d in range(1, n_blk):
            seed_copy(d, r).start()

    send_seeds(farthest)

    edges(xfull, half)
    xfull[near, :] = x_ref[:, mine].astype(jnp.float32)
    swap.wait_recv()
    xfull[far_rows, :] = xrecv[...].astype(jnp.float32)
    lag_own = jnp.where(tm == 0, jnp.concatenate(lag_rows[:groups], axis=1),
                        jnp.concatenate(lag_rows[groups:], axis=1))
    for g in range(groups):
        lagscr[g:g + 1, :] = lag_own[:, g * 128:(g + 1) * 128]

    i = lax.broadcasted_iota(jnp.int32, (rows_run, rows_run), 0)
    j = lax.broadcasted_iota(jnp.int32, (rows_run, rows_run), 1)
    n_vec = jnp.full((rows_run, rows_run), n_blk, jnp.int32)
    order = one_hot(j == lax.rem(i, n_vec) * q_run + lax.div(i, n_vec))

    def prepare(r):
        for d in range(1, n_blk):
            arrived(d, r)
        rows_left = jnp.concatenate([seeds[b, r] for b in range(n_blk)], axis=0)
        left[...] = jnp.dot(order, rows_left, preferred_element_type=jnp.float32).astype(jnp.bfloat16)

    def corr(p):
        cols = pl.ds(pl.multiple_of(p * WIDE, WIDE), WIDE)
        return jnp.dot(left[...], scores[:, cols], preferred_element_type=jnp.float32) / total

    def encode(buf, at, v):
        count = v.shape[0]
        peak = jnp.max(jnp.abs(v), axis=0, keepdims=True)
        lane = jnp.maximum(peak[:, 0:128], peak[:, 128:256])
        code = jnp.ceil(jnp.log2(jnp.maximum(lane, 1e-30)) * STEPS) + 1.0
        gain = TOP * jnp.exp2(code * (-1.0 / STEPS))
        for g in range(2):
            scaled = jnp.round(v[:, g * 128:(g + 1) * 128] * gain)
            buf[at + g * count:at + (g + 1) * count, :] = scaled.astype(jnp.int32).astype(jnp.int16)
        at += 2 * count
        buf[at:at + 16, :] = jnp.broadcast_to(code, (16, 128)).astype(jnp.int32).astype(jnp.int16)

    def decode(buf, count):
        code = buf[2 * count:2 * count + 16, :].astype(jnp.int32).astype(jnp.float32)[0:1, :]
        unit = jnp.exp2(code * (1.0 / STEPS)) * (1.0 / TOP)
        return jnp.concatenate(
            [buf[g * count:(g + 1) * count, :].astype(jnp.int32).astype(jnp.float32) * unit for g in range(2)],
            axis=1)

    long, short = 2 * rows_run + 16, 2 * rows + 16

    def pass_on(r, p):
        nxt = jnp.where(r > z, z + 1, z - 1)
        return pltpu.make_async_remote_copy(
            src_ref=stage.at[r, p, pl.ds(0, long)], dst_ref=transit.at[r, p], send_sem=tsend.at[r, p, 0],
            recv_sem=trecv.at[r, p], device_id=dev(nxt, tm, blk), device_id_type=mesh_id)

    def deliver(r, p, h):
        way = jnp.where(r > z, 0, 1)
        return pltpu.make_async_remote_copy(
            src_ref=stage.at[r, p, pl.ds(h * short, short)], dst_ref=final.at[way, tm, p],
            send_sem=tsend.at[r, p, h], recv_sem=frecv.at[way, tm, p],
            device_id=dev(r, h, blk), device_id_type=mesh_id)

    def send_block(r, p):
        up = r > z
        nxt = jnp.where(up, z + 1, z - 1)
        part[...] = corr(p)

        @pl.when(jnp.logical_or(jnp.logical_and(up, z > 0), jnp.logical_and(r < z, z < n_run - 1)))
        def _():
            pltpu.make_async_copy(transit.at[r, p], transit.at[r, p], trecv.at[r, p]).wait()
            part[...] += decode(transit.at[r, p], rows_run)

        def after():
            @pl.when(jnp.logical_and(r != 0, r != n_run - 1))
            def _():
                pass_on(jnp.where(up, r + 1, r - 1), p).wait_send()

        @pl.when(r == nxt)
        def _():
            for h in range(2):
                encode(stage.at[r, p], h * short, part[h * rows:(h + 1) * rows, :])
            after()
            for h in range(2):
                deliver(r, p, h).start()

        @pl.when(r != nxt)
        def _():
            encode(stage.at[r, p], 0, part[...])
            after()
            pass_on(r, p).start()

    n_wide = half // WIDE
    late = (zz > 0).astype(jnp.int32)

    def pair(p, carry):
        @pl.when(p < n_wide)
        def _():
            lane0 = pl.multiple_of(p * WIDE, WIDE)
            lag = jnp.concatenate([lagscr[pl.ds(2 * p, 1), :], lagscr[pl.ds(2 * p + 1, 1), :]], axis=1)

            def store(r0, g, v):
                scores[r0:r0 + CHUNK, pl.ds(pl.multiple_of(lane0 + g * 128, 128), 128)] = v

            normalize(xfull, pl.ds(lane0, WIDE), lag, store)

        @pl.when(p == 0)
        def _():
            send_seeds(turn(1))

        @pl.when(p == 1)
        def _():
            def send_rest(j, carry):
                send_seeds(turn(j))
                return carry

            lax.fori_loop(2, n_run, send_rest, 0)

        t = p - late

        @pl.when(t == 0)
        def _():
            prepare(farthest)

        @pl.when(jnp.logical_and(t >= 0, t < n_wide))
        def _():
            send_block(farthest, t)

        return carry

    lax.fori_loop(0, n_wide + 1, pair, 0)

    def send_run(j, carry):
        r = turn(j)

        prepare(r)

        def wide(p, carry):
            send_block(r, p)
            return carry

        lax.fori_loop(0, n_wide, wide, 0)
        return carry

    lax.fori_loop(1, n_run - 1, send_run, 0)

    prepare(z)
    for p in range(n_wide):
        own[:, p * WIDE:(p + 1) * WIDE] = corr(p)
    keep = pl.ds(pl.multiple_of(tm * rows, rows), rows)
    give = pl.ds(pl.multiple_of(other * rows, rows), rows)
    trade = pltpu.make_async_remote_copy(
        src_ref=own.at[give, :], dst_ref=ownrecv, send_sem=osem.at[0], recv_sem=osem.at[1],
        device_id=dev(z, other, blk), device_id_type=mesh_id)
    trade.start()
    out_ref[:, mine] = own[keep, :] / n_run
    trade.wait_recv()
    out_ref[:, theirs] = ownrecv[...] / n_run
    for way, present in ((0, z > 0), (1, z < n_run - 1)):

        @pl.when(present)
        def _():
            for p in range(n_wide):
                for c in range(2):
                    pltpu.make_async_copy(final.at[way, c, p], final.at[way, c, p], frecv.at[way, c, p]).wait()
                    cols = slice(c * half + p * WIDE, c * half + (p + 1) * WIDE)
                    out_ref[:, cols] += decode(final.at[way, c, p], rows) / n_run

    sswap.wait_send()
    swap.wait_send()
    trade.wait_send()

    def drain(r, carry):
        for d in range(1, n_blk):
            seed_copy(d, r).wait_send()

        @pl.when(jnp.logical_or(r == z - 1, r == z + 1))
        def _():
            for p in range(n_wide):
                for h in range(2):
                    deliver(r, p, h).wait_send()

        return carry

    lax.fori_loop(0, n_run, drain, 0)


def local(n_run, n_blk, series, weights, taps, lags):
    signal = series[0]
    frames, panel = signal.shape
    half = panel // 2
    fp = -(-2 * frames // 256) * 256
    n_filter = -(-(fp + LAGS) // OUT_BLK)
    rows_run = SEED_DEV // n_run * n_blk
    rows = rows_run // 2
    long, short = 2 * rows_run + 16, 2 * rows + 16
    n_wide = half // WIDE
    vmem = pl.BlockSpec(memory_space=pltpu.VMEM)
    dma = pltpu.SemaphoreType.DMA
    f32, b16 = jnp.float32, jnp.bfloat16
    flops = 2 * half * fp * (IN_BLK + n_blk * SEED_DEV)
    return pl.pallas_call(
        functools.partial(kernel, (n_run, n_blk, frames, panel, fp, n_filter)),
        out_shape=pltpu.VMEM((rows, panel), f32),
        in_specs=[pl.BlockSpec(memory_space=pl.ANY), vmem, pl.BlockSpec(memory_space=pltpu.SMEM), vmem],
        out_specs=vmem,
        scratch_shapes=[
            pltpu.VMEM((frames, panel), b16),
            pltpu.VMEM((frames, SEED_DEV), b16),
            pltpu.VMEM((frames, SEED_DEV), b16),
            pltpu.VMEM((n_filter * OUT_BLK + IN_BLK - OUT_BLK, SEED_DEV), f32),
            pltpu.VMEM((fp, SEED_DEV), b16),
            pltpu.VMEM((frames, half), b16),
            pltpu.VMEM((n_filter * OUT_BLK + IN_BLK - OUT_BLK, half), f32),
            pltpu.VMEM((OUT_BLK, IN_BLK), b16),
            pltpu.VMEM((fp, 128), f32),
            pltpu.VMEM((fp, 128), f32),
            pltpu.VMEM((half // 128, 128), jnp.int32),
            pltpu.VMEM((n_filter * OUT_BLK, 256), f32),
            pltpu.VMEM((fp, 256), f32),
            pltpu.VMEM((fp, half), b16),
            pltpu.VMEM((n_blk, n_run, SEED_DEV // n_run, fp), b16),
            pltpu.VMEM((rows_run, fp), b16),
            pltpu.VMEM((n_run, n_wide, 2 * short, 128), jnp.int16),
            pltpu.VMEM((n_run, n_wide, long, 128), jnp.int16),
            pltpu.VMEM((2, 2, n_wide, short, 128), jnp.int16),
            pltpu.VMEM((rows_run, WIDE), f32),
            pltpu.VMEM((rows_run, half), f32),
            pltpu.VMEM((rows, half), f32),
            dma((5,)),
            dma((n_blk, n_run)),
            dma((n_blk, n_run)),
            dma((n_run, n_wide, 2)),
            dma((n_run, n_wide)),
            dma((2, 2, n_wide)),
            dma((2,)),
        ],
        compiler_params=pltpu.CompilerParams(
            collective_id=0, has_side_effects=True, vmem_limit_bytes=56 * 1024 * 1024),
        cost_estimate=pl.CostEstimate(flops=flops, bytes_accessed=2 * frames * panel, transcendentals=0),
    )(signal, weights, taps, lags.reshape(panel // 128, 128))


def solution(mesh):
    placed = (P("run", "tm", "blk"), P("run", None), P(), P("blk"))
    body = functools.partial(local, mesh.shape["run"], mesh.shape["blk"])
    return jax.shard_map(
        body, mesh=mesh, in_specs=placed, out_specs=P(("run", "tm"), "blk"), check_vma=False
    )
```

```python
import functools

import jax
import jax.numpy as jnp
from jax import lax
from jax.experimental import pallas as pl
from jax.experimental.pallas import tpu as pltpu
from jax.sharding import PartitionSpec as P

HALF = 16
LAGS = 4
SEED_DEV = 128
TAPS = 2 * HALF + 1
OUT_BLK = 224
IN_BLK = 256
CHUNK = 128
WIDE = 256
TOP = 32000.0
STEPS = 128.0
epsilon = 1e-05


def kernel(dims, x_hbm, w_hbm, taps_hbm, lags_hbm, out_ref, w_ref, taps_ref, lags_ref, x_ref, sown, sother, sfull, sscore, xrecv, xfull, toep, wcol,
           rcol, lagscr, banded, filt, scores, seeds, left, stage, transit, final, part, own, ownrecv, xsem, dsend, srecv, tsend,
           trecv, frecv, osem):
    n_run, n_blk, frames, panel, fp, n_filter = dims
    half = panel // 2
    groups = half // 128
    total_frames = 2 * frames
    q_run = SEED_DEV // n_run
    rows_run = q_run * n_blk
    rows = rows_run // 2
    runs_core = n_run // 2

    z = lax.axis_index("run")
    tm = lax.axis_index("tm")
    blk = lax.axis_index("blk")
    other = 1 - tm

    def dev(run, core, block):
        return (run, core, block)

    barrier = pltpu.get_barrier_semaphore()
    mesh_id = pl.DeviceIdType.MESH
    pl.semaphore_signal(barrier, inc=1, device_id=dev(z, other, blk), device_id_type=mesh_id)
    for d in range(1, n_blk):
        peer = lax.rem(blk + d, n_blk)
        pl.semaphore_signal(barrier, inc=1, device_id=dev(z, tm, peer), device_id_type=mesh_id)

    @pl.when(z > 0)
    def _():
        for core in range(2):
            pl.semaphore_signal(barrier, inc=1, device_id=dev(z - 1, core, blk), device_id_type=mesh_id)

    @pl.when(z < n_run - 1)
    def _():
        for core in range(2):
            pl.semaphore_signal(barrier, inc=1, device_id=dev(z + 1, core, blk), device_id_type=mesh_id)

    mine = pl.ds(pl.multiple_of(tm * half, 128), half)
    theirs = pl.ds(pl.multiple_of(other * half, 128), half)
    loads = [pltpu.make_async_copy(w_hbm, w_ref, xsem.at[4])]
    for c in range(2):
        cols = slice(c * half, (c + 1) * half)
        loads.append(pltpu.make_async_copy(x_hbm.at[:, cols], x_ref.at[:, cols], xsem.at[5 + c]))
    loads.append(pltpu.make_async_copy(taps_hbm, taps_ref, xsem.at[7]))
    loads.append(pltpu.make_async_copy(lags_hbm, lags_ref, xsem.at[8]))
    for load in loads:
        load.start()
    loads[0].wait()

    wrow = w_ref[...].astype(jnp.float32)
    total = jnp.sum(wrow)
    wrow = jnp.concatenate([wrow, jnp.zeros((1, fp - total_frames), jnp.float32)], axis=1)
    for j in range(fp // 128):
        square = jnp.broadcast_to(wrow[:, j * 128:(j + 1) * 128], (128, 128)).T
        wcol[j * 128:(j + 1) * 128, :] = square
        rcol[j * 128:(j + 1) * 128, :] = jnp.sqrt(square)

    def one_hot(mask):
        return mask.astype(jnp.float32).astype(jnp.bfloat16)

    pick = one_hot(lax.broadcasted_iota(jnp.int32, (panel, SEED_DEV), 0)
                   == (panel // SEED_DEV) * lax.broadcasted_iota(jnp.int32, (panel, SEED_DEV), 1))
    picked = jnp.zeros((frames, SEED_DEV), jnp.float32)
    for c in range(2):
        loads[1 + c].wait()
        cols = slice(c * half, (c + 1) * half)
        picked = picked + jnp.dot(x_ref[:, cols], pick[cols], preferred_element_type=jnp.float32)
    sown[...] = picked.astype(jnp.bfloat16)

    inner = jnp.logical_and(z > 0, z < n_run - 1)
    pl.semaphore_wait(barrier, jnp.where(inner, n_blk + 4, n_blk + 2))

    sswap = pltpu.make_async_remote_copy(
        src_ref=sown, dst_ref=sother, send_sem=xsem.at[2], recv_sem=xsem.at[3],
        device_id=dev(z, other, blk), device_id_type=mesh_id)
    sswap.start()
    swap = pltpu.make_async_remote_copy(
        src_ref=x_ref.at[:, theirs], dst_ref=xrecv, send_sem=xsem.at[0], recv_sem=xsem.at[1],
        device_id=dev(z, other, blk), device_id_type=mesh_id)
    swap.start()

    loads[3].wait()
    loads[4].wait()
    lane = lax.broadcasted_iota(jnp.int32, (8, IN_BLK), 1)
    row = jnp.zeros((8, IN_BLK), jnp.float32)
    for k in range(TAPS):
        row = jnp.where(lane == k, taps_ref[k].astype(jnp.float32), row)
    band = jnp.broadcast_to(row[0:1, :], (OUT_BLK, IN_BLK))
    toep[...] = pltpu.roll(band, 0, 1, stride=1, stride_axis=0).astype(jnp.bfloat16)

    tail = HALF + total_frames
    near = pl.ds(pl.multiple_of(HALF + tm * frames, 8), frames)
    far_rows = pl.ds(pl.multiple_of(HALF + other * frames, 8), frames)

    def edges(ref, width):
        ref[0:HALF, :] = jnp.zeros((HALF, width), jnp.float32)
        ref[tail:, :] = jnp.zeros((ref.shape[0] - tail, width), jnp.float32)

    def normalize(src, lanes, lag, dst):
        width = lag.shape[1]
        for b in range(n_filter):
            banded[b * OUT_BLK:(b + 1) * OUT_BLK, 0:width] = jnp.dot(
                toep[...], src[b * OUT_BLK:b * OUT_BLK + IN_BLK, lanes].astype(jnp.bfloat16),
                preferred_element_type=jnp.float32)
        for g in range(width // 128):
            part = slice(g * 128, (g + 1) * 128)
            odd = jnp.broadcast_to((lag[:, part] & 1) == 1, (CHUNK + 8, 128))
            high = jnp.broadcast_to(lag[:, part] >= 2, (CHUNK, 128))
            sums = []
            for r0 in range(0, fp, CHUNK):
                late = banded[r0:r0 + CHUNK + 16, part]
                v = jnp.where(odd, late[1:CHUNK + 9], late[0:CHUNK + 8])
                v = jnp.where(high, v[2:CHUNK + 2], v[0:CHUNK])
                v = v.astype(jnp.bfloat16).astype(jnp.float32)
                filt[r0:r0 + CHUNK, part] = v
                wv = wcol[r0:r0 + CHUNK, :] * v
                sums.append((jnp.sum(wv.reshape(CHUNK // 8, 8, 128), axis=0),
                             jnp.sum((wv * v).reshape(CHUNK // 8, 8, 128), axis=0)))
            first = jnp.sum(sum(a for a, _ in sums), axis=0, keepdims=True) / total
            second = jnp.sum(sum(a for _, a in sums), axis=0, keepdims=True) / total
            scaling = lax.rsqrt(second - first * first + epsilon)
            for r0 in range(0, fp, CHUNK):
                v = rcol[r0:r0 + CHUNK, :] * (filt[r0:r0 + CHUNK, part] - first) * scaling
                dst(r0, g, v.astype(jnp.bfloat16))

    edges(sfull, SEED_DEV)
    sfull[near, :] = sown[...].astype(jnp.float32)
    lag_rows = [lags_ref[j:j + 1, :] for j in range(panel // 128)]
    lag_all = jnp.broadcast_to(jnp.concatenate(lag_rows, axis=1), (8, panel)).astype(jnp.float32)
    seed_lag = jnp.dot(lag_all.astype(jnp.bfloat16), pick, preferred_element_type=jnp.float32)
    seed_lag = seed_lag.astype(jnp.int32)[0:1, :]
    sswap.wait_recv()
    sfull[far_rows, :] = sother[...].astype(jnp.float32)

    def seed_store(r0, g, v):
        sscore[r0:r0 + CHUNK, :] = v

    normalize(sfull, slice(0, SEED_DEV), seed_lag, seed_store)
    eye = one_hot(lax.broadcasted_iota(jnp.int32, (SEED_DEV, SEED_DEV), 1)
                  == lax.broadcasted_iota(jnp.int32, (SEED_DEV, SEED_DEV), 0))
    rows_seed = lax.dot_general(
        eye, sscore[...], (((1,), (1,)), ((), ())), preferred_element_type=jnp.float32).astype(jnp.bfloat16)
    for r in range(n_run):
        seeds[blk, r] = rows_seed[r * q_run:(r + 1) * q_run, :]

    flip = (z >= runs_core).astype(jnp.int32)
    zz = z + flip * (n_run - 1 - 2 * z)

    def unflip(rr):
        return rr + flip * (n_run - 1 - 2 * rr)

    def turn(j):
        pairs = jnp.where(lax.rem(j, 2) == 0, n_run - 1 - lax.div(j, 2), lax.div(j, 2))
        return unflip(jnp.where(j < 2 * zz, pairs, n_run - 1 - j + zz))

    farthest = unflip(n_run - 1)

    def seed_copy(d, r):
        return pltpu.make_async_remote_copy(
            src_ref=seeds.at[blk, r], dst_ref=seeds.at[blk, r], send_sem=dsend.at[d, r],
            recv_sem=srecv.at[blk, r], device_id=dev(z, tm, lax.rem(blk + d, n_blk)), device_id_type=mesh_id)

    def arrived(d, r):
        peer = lax.rem(blk + n_blk - d, n_blk)
        pltpu.make_async_copy(seeds.at[peer, r], seeds.at[peer, r], srecv.at[peer, r]).wait()

    def send_seeds(r):
        for d in range(1, n_blk):
            seed_copy(d, r).start()

    send_seeds(farthest)

    edges(xfull, half)
    xfull[near, :] = x_ref[:, mine].astype(jnp.float32)
    swap.wait_recv()
    xfull[far_rows, :] = xrecv[...].astype(jnp.float32)
    lag_own = jnp.where(tm == 0, jnp.concatenate(lag_rows[:groups], axis=1),
                        jnp.concatenate(lag_rows[groups:], axis=1))
    for g in range(groups):
        lagscr[g:g + 1, :] = lag_own[:, g * 128:(g + 1) * 128]

    i = lax.broadcasted_iota(jnp.int32, (rows_run, rows_run), 0)
    j = lax.broadcasted_iota(jnp.int32, (rows_run, rows_run), 1)
    n_vec = jnp.full((rows_run, rows_run), n_blk, jnp.int32)
    order = one_hot(j == lax.rem(i, n_vec) * q_run + lax.div(i, n_vec))

    def prepare(r):
        for d in range(1, n_blk):
            arrived(d, r)
        rows_left = jnp.concatenate([seeds[b, r] for b in range(n_blk)], axis=0)
        left[...] = jnp.dot(order, rows_left, preferred_element_type=jnp.float32).astype(jnp.bfloat16)

    def corr(p):
        cols = pl.ds(pl.multiple_of(p * WIDE, WIDE), WIDE)
        return jnp.dot(left[...], scores[:, cols], preferred_element_type=jnp.float32) / total

    def encode(buf, at, v):
        count = v.shape[0]
        peak = jnp.max(jnp.abs(v), axis=0, keepdims=True)
        lane = jnp.maximum(peak[:, 0:128], peak[:, 128:256])
        code = jnp.ceil(jnp.log2(jnp.maximum(lane, 1e-30)) * STEPS) + 1.0
        gain = TOP * jnp.exp2(code * (-1.0 / STEPS))
        for g in range(2):
            scaled = jnp.round(v[:, g * 128:(g + 1) * 128] * gain)
            buf[at + g * count:at + (g + 1) * count, :] = scaled.astype(jnp.int32).astype(jnp.int16)
        at += 2 * count
        buf[at:at + 16, :] = jnp.broadcast_to(code, (16, 128)).astype(jnp.int32).astype(jnp.int16)

    def decode(buf, count):
        code = buf[2 * count:2 * count + 16, :].astype(jnp.int32).astype(jnp.float32)[0:1, :]
        unit = jnp.exp2(code * (1.0 / STEPS)) * (1.0 / TOP)
        return jnp.concatenate(
            [buf[g * count:(g + 1) * count, :].astype(jnp.int32).astype(jnp.float32) * unit for g in range(2)],
            axis=1)

    long, short = 2 * rows_run + 16, 2 * rows + 16

    def pass_on(r, p):
        nxt = jnp.where(r > z, z + 1, z - 1)
        return pltpu.make_async_remote_copy(
            src_ref=stage.at[r, p, pl.ds(0, long)], dst_ref=transit.at[r, p], send_sem=tsend.at[r, p, 0],
            recv_sem=trecv.at[r, p], device_id=dev(nxt, tm, blk), device_id_type=mesh_id)

    def deliver(r, p, h):
        way = jnp.where(r > z, 0, 1)
        return pltpu.make_async_remote_copy(
            src_ref=stage.at[r, p, pl.ds(h * short, short)], dst_ref=final.at[way, tm, p],
            send_sem=tsend.at[r, p, h], recv_sem=frecv.at[way, tm, p],
            device_id=dev(r, h, blk), device_id_type=mesh_id)

    def send_block(r, p):
        up = r > z
        nxt = jnp.where(up, z + 1, z - 1)
        part[...] = corr(p)

        @pl.when(jnp.logical_or(jnp.logical_and(up, z > 0), jnp.logical_and(r < z, z < n_run - 1)))
        def _():
            pltpu.make_async_copy(transit.at[r, p], transit.at[r, p], trecv.at[r, p]).wait()
            part[...] += decode(transit.at[r, p], rows_run)

        def after():
            @pl.when(jnp.logical_and(r != 0, r != n_run - 1))
            def _():
                pass_on(jnp.where(up, r + 1, r - 1), p).wait_send()

        @pl.when(r == nxt)
        def _():
            for h in range(2):
                encode(stage.at[r, p], h * short, part[h * rows:(h + 1) * rows, :])
            after()
            for h in range(2):
                deliver(r, p, h).start()

        @pl.when(r != nxt)
        def _():
            encode(stage.at[r, p], 0, part[...])
            after()
            pass_on(r, p).start()

    n_wide = half // WIDE
    begin = jnp.where(zz > 0, n_wide - 1, min(1, n_wide - 1))

    def send_farthest(t, carry):
        send_block(farthest, t)
        return carry

    def pair(p, carry):
        lane0 = pl.multiple_of(p * WIDE, WIDE)
        lag = jnp.concatenate([lagscr[pl.ds(2 * p, 1), :], lagscr[pl.ds(2 * p + 1, 1), :]], axis=1)

        def store(r0, g, v):
            scores[r0:r0 + CHUNK, pl.ds(pl.multiple_of(lane0 + g * 128, 128), 128)] = v

        normalize(xfull, pl.ds(lane0, WIDE), lag, store)

        @pl.when(p == 0)
        def _():
            send_seeds(turn(1))

        @pl.when(p == min(1, n_wide - 1))
        def _():
            def send_rest(j, carry):
                send_seeds(turn(j))
                return carry

            lax.fori_loop(2, n_run, send_rest, 0)

        @pl.when(p == begin)
        def _():
            prepare(farthest)

        @pl.when(p >= begin)
        def _():
            lax.fori_loop(jnp.where(p == begin, 0, p), p + 1, send_farthest, 0)

        return carry

    lax.fori_loop(0, n_wide, pair, 0)

    def send_run(j, carry):
        r = turn(j)

        prepare(r)

        def wide(p, carry):
            send_block(r, p)
            return carry

        lax.fori_loop(0, n_wide, wide, 0)
        return carry

    lax.fori_loop(1, n_run - 1, send_run, 0)

    prepare(z)
    for p in range(n_wide):
        own[:, p * WIDE:(p + 1) * WIDE] = corr(p)
    keep = pl.ds(pl.multiple_of(tm * rows, rows), rows)
    give = pl.ds(pl.multiple_of(other * rows, rows), rows)
    trade = pltpu.make_async_remote_copy(
        src_ref=own.at[give, :], dst_ref=ownrecv, send_sem=osem.at[0], recv_sem=osem.at[1],
        device_id=dev(z, other, blk), device_id_type=mesh_id)
    trade.start()
    out_ref[:, mine] = own[keep, :] / n_run
    trade.wait_recv()
    out_ref[:, theirs] = ownrecv[...] / n_run
    for way, present in ((0, z > 0), (1, z < n_run - 1)):

        @pl.when(present)
        def _():
            for p in range(n_wide):
                for c in range(2):
                    pltpu.make_async_copy(final.at[way, c, p], final.at[way, c, p], frecv.at[way, c, p]).wait()
                    cols = slice(c * half + p * WIDE, c * half + (p + 1) * WIDE)
                    out_ref[:, cols] += decode(final.at[way, c, p], rows) / n_run

    sswap.wait_send()
    swap.wait_send()
    trade.wait_send()

    def drain(r, carry):
        for d in range(1, n_blk):
            seed_copy(d, r).wait_send()

        @pl.when(jnp.logical_or(r == z - 1, r == z + 1))
        def _():
            for p in range(n_wide):
                for h in range(2):
                    deliver(r, p, h).wait_send()

        return carry

    lax.fori_loop(0, n_run, drain, 0)


def local(n_run, n_blk, series, weights, taps, lags):
    signal = series[0]
    frames, panel = signal.shape
    half = panel // 2
    fp = -(-2 * frames // 256) * 256
    n_filter = -(-(fp + LAGS) // OUT_BLK)
    rows_run = SEED_DEV // n_run * n_blk
    rows = rows_run // 2
    long, short = 2 * rows_run + 16, 2 * rows + 16
    n_wide = half // WIDE
    vmem = pl.BlockSpec(memory_space=pltpu.VMEM)
    dma = pltpu.SemaphoreType.DMA
    f32, b16 = jnp.float32, jnp.bfloat16
    flops = 2 * half * fp * (IN_BLK + n_blk * SEED_DEV)
    return pl.pallas_call(
        functools.partial(kernel, (n_run, n_blk, frames, panel, fp, n_filter)),
        out_shape=pltpu.VMEM((rows, panel), f32),
        in_specs=[pl.BlockSpec(memory_space=pl.ANY)] * 4,
        out_specs=vmem,
        scratch_shapes=[
            pltpu.VMEM(weights.shape, jnp.int32),
            pltpu.SMEM(taps.shape, b16),
            pltpu.VMEM((panel // 128, 128), jnp.int32),
            pltpu.VMEM((frames, panel), b16),
            pltpu.VMEM((frames, SEED_DEV), b16),
            pltpu.VMEM((frames, SEED_DEV), b16),
            pltpu.VMEM((n_filter * OUT_BLK + IN_BLK - OUT_BLK, SEED_DEV), f32),
            pltpu.VMEM((fp, SEED_DEV), b16),
            pltpu.VMEM((frames, half), b16),
            pltpu.VMEM((n_filter * OUT_BLK + IN_BLK - OUT_BLK, half), f32),
            pltpu.VMEM((OUT_BLK, IN_BLK), b16),
            pltpu.VMEM((fp, 128), f32),
            pltpu.VMEM((fp, 128), f32),
            pltpu.VMEM((half // 128, 128), jnp.int32),
            pltpu.VMEM((n_filter * OUT_BLK, 256), f32),
            pltpu.VMEM((fp, 256), f32),
            pltpu.VMEM((fp, half), b16),
            pltpu.VMEM((n_blk, n_run, SEED_DEV // n_run, fp), b16),
            pltpu.VMEM((rows_run, fp), b16),
            pltpu.VMEM((n_run, n_wide, 2 * short, 128), jnp.int16),
            pltpu.VMEM((n_run, n_wide, long, 128), jnp.int16),
            pltpu.VMEM((2, 2, n_wide, short, 128), jnp.int16),
            pltpu.VMEM((rows_run, WIDE), f32),
            pltpu.VMEM((rows_run, half), f32),
            pltpu.VMEM((rows, half), f32),
            dma((9,)),
            dma((n_blk, n_run)),
            dma((n_blk, n_run)),
            dma((n_run, n_wide, 2)),
            dma((n_run, n_wide)),
            dma((2, 2, n_wide)),
            dma((2,)),
        ],
        compiler_params=pltpu.CompilerParams(
            collective_id=0, has_side_effects=True, vmem_limit_bytes=56 * 1024 * 1024),
        cost_estimate=pl.CostEstimate(flops=flops, bytes_accessed=2 * frames * panel, transcendentals=0),
    )(signal, weights, taps, lags.reshape(panel // 128, 128))


def solution(mesh):
    placed = (P("run", "tm", "blk"), P("run", None), P(), P("blk"))
    body = functools.partial(local, mesh.shape["run"], mesh.shape["blk"])
    return jax.shard_map(
        body, mesh=mesh, in_specs=placed, out_specs=P(("run", "tm"), "blk"), check_vma=False
    )
```
